32 devices in a mesh: expert: 4 (over z), shard: 8 (over y, x, core).
Axes of the slice: x: 2, y: 2, z: 4, core: 2. Of those that a mesh axis runs over, the one named last changes fastest.
Arguments:
- tokens: bfloat16 [32768, 768], P(('expert', 'shard')), may hold values from -6 to 6
- cotangent: bfloat16 [32768, 768], P(('expert', 'shard')), may hold values from -6 to 6
- prev_logits: float32 [32768, 12], P(('expert', 'shard')), may hold values from -3 to 3
- routes: int32 [32768, 2], P(('expert', 'shard')), may hold values from 0 to 11, all different within a row
- priority: int32 [32, 2048], P(('expert', 'shard')), may hold values from 0 to 2047, each once within a row
- gain_mix: bfloat16 [768], P('shard'), may hold values from 0.5 to 1.5
- mix_qkv: bfloat16 [768, 2304], P('shard'), may hold values from -0.21875 to 0.21875
- mix_out: bfloat16 [768, 768], P('shard'), may hold values from -3.59375 to 3.59375
- gain_moe: bfloat16 [768], P('shard'), may hold values from 0.5 to 1.5
- router: bfloat16 [768, 12], P('shard'), may hold values from -0.109375 to 0.109375
- constants: bfloat16 [768, 2], P('shard'), may hold values from -6 to 6
- w_gate: bfloat16 [8, 768, 2048], P('expert', None, 'shard'), may hold values from -0.21875 to 0.21875
- w_up: bfloat16 [8, 768, 2048], P('expert', None, 'shard'), may hold values from -0.21875 to 0.21875
- w_down: bfloat16 [8, 768, 2048], P('expert', None, 'shard'), may hold values from -0.125 to 0.125
Outputs:
- block_out: bfloat16 [32768, 768], P(('expert', 'shard'))
- token_grad: float32 [32768, 768], P(('expert', 'shard'))
- logit_grad: float32 [32768, 12], P(('expert', 'shard'))
- grad_gain_mix: float32 [768], P('shard')
- grad_qkv: float32 [768, 2304], P('shard')
- grad_out: float32 [768, 768], P('shard')
- grad_gain_moe: float32 [768], P('shard')
- grad_router: float32 [768, 12], P('shard')
- grad_constants: float32 [768, 2], P('shard')
- grad_gate: float32 [8, 768, 2048], P('expert', None, 'shard')
- grad_up: float32 [8, 768, 2048], P('expert', None, 'shard')
- grad_down: float32 [8, 768, 2048], P('expert', None, 'shard')
The draws below stay inside these ranges and needn't reach their ends.
Inputs may be any that keep to these rules, and one draw needn't show every extreme that they name: `routes`: each row names two different experts, and every expert is named by some row. `priority`: each row is a permutation: the claim order of the 2048 pairs of one sequence, pair 2 t + j being the sequence's token t with its j-th route.
All inputs are finite; a program needn't handle non-finite values.
Results may differ from the reference program's by a relative error of at most 0.03.
Values may be sent and summed in bfloat16 or wider, within the bound.
No kernel may reach another device: no remote copies, remote signals or barrier semaphores. Data moves between devices by JAX's collectives and lax.ppermute only.
A program may use at most 256 MiB of HBM per device.

```python
import jax
import jax.numpy as jnp
from jax import lax

D = 768
HEADS = 12
HEAD = 64
FF = 2048
EXPERTS = 8
ZEROS = 4
TOP = 2
BLOCK = 256
TOK_DEV = 1024
ALL = 12
CAP = 216
TOKENS = 32768


def block_scale(key, dims, cuts, smallest, high):
    factor_of = 1.0
    for dim, shards_of in cuts:
        heights = jax.random.uniform(jax.random.fold_in(jax.random.fold_in(key, 6), dim), (shards_of,), jnp.float32, smallest / len(cuts), high / len(cuts))
        factor_of = factor_of * jnp.repeat(jnp.exp(heights), dims[dim] // shards_of).reshape((-1,) + (1,) * (len(dims) - 1 - dim))
    return factor_of


def choose_distinct(key, rows, number_of, top, lift):
    order = jax.random.permutation(jax.random.fold_in(key, 1), number_of)
    favour = order
    for power in range(3):
        favour = favour * favour // number_of
    favour = favour * lift // number_of
    lots = jax.random.randint(jax.random.fold_in(key, 2), (rows, number_of), 0, 4096) + favour
    holders = jax.random.permutation(jax.random.fold_in(key, 3), rows)[jnp.arange(number_of) % rows]
    lots = jnp.where(jnp.arange(rows)[:, None] == holders[None, :], 1 << 14, lots)
    score = lots * number_of + jnp.arange(number_of)
    return lax.top_k(score.astype(jnp.int32), top)[1].astype(jnp.int32)


def scatter_about(stream_key, shape, spread, bound, split=(), kind=jnp.bfloat16):
    gain = block_scale(stream_key, shape, split, -0.22, 0.18) if split else 1.0
    drawn = jax.random.normal(stream_key, shape, jnp.float32) * spread * gain
    return jnp.minimum(jnp.maximum(drawn, -bound), bound).astype(kind)


def setup_inputs(seed: int = 0) -> dict:
    streams_of = jax.random.split(jax.random.key(seed), 15)
    return {
        "tokens": scatter_about(streams_of[0], (TOKENS, D), 1.0, 6.0, ((0, 32),)),
        "cotangent": scatter_about(streams_of[1], (TOKENS, D), 1.0, 6.0, ((0, 32),)),
        "prev_logits": scatter_about(streams_of[2], (TOKENS, ALL), 0.5, 3.0, ((0, 32),), jnp.float32),
        "routes": choose_distinct(streams_of[3], TOKENS, ALL, TOP, 1365),
        "priority": jax.vmap(lambda own: jax.random.permutation(own, TOP * TOK_DEV))(jax.random.split(streams_of[4], (TOKENS // TOK_DEV))).reshape((TOKENS // TOK_DEV, TOP * TOK_DEV)).astype(jnp.int32),
        "gain_mix": jnp.clip(1.0 + 0.1 * jax.random.normal(streams_of[5], (D,), jnp.float32), 0.5, 1.5).astype(jnp.bfloat16),
        "mix_qkv": scatter_about(streams_of[6], (D, 3 * D), D ** -0.5, 0.21875, ((0, 8),)),
        "mix_out": scatter_about(streams_of[7], (D, D), 0.6, 3.59375, ((0, 8),)),
        "gain_moe": jnp.clip(1.0 + 0.1 * jax.random.normal(streams_of[8], (D,), jnp.float32), 0.5, 1.5).astype(jnp.bfloat16),
        "router": scatter_about(streams_of[9], (D, ALL), (4 * D) ** -0.5, 0.109375, ((0, 8),)),
        "constants": scatter_about(streams_of[10], (D, 2), 1.0, 6.0, ((0, 8),)),
        "w_gate": scatter_about(streams_of[11], (EXPERTS, D, FF), D ** -0.5, 0.21875, ((0, 4), (2, 8))),
        "w_up": scatter_about(streams_of[12], (EXPERTS, D, FF), D ** -0.5, 0.21875, ((0, 4), (2, 8))),
        "w_down": scatter_about(streams_of[13], (EXPERTS, D, FF), FF ** -0.5, 0.125, ((0, 4), (2, 8))),
    }


@jax.custom_vjp
def low(v):
    return lax.optimization_barrier(v.astype(jnp.bfloat16)).astype(jnp.float32)

@jax.custom_vjp
def low_back(v):
    return v

def low_keep(v):
    return (low(v), None)

def low_pass(kept, grad):
    return (grad,)

def back_keep(v):
    return (v, None)

def back_low(kept, grad):
    return (low(grad),)
low.defvjp(low_keep, low_pass)
low_back.defvjp(back_keep, back_low)
epsilon = 1e-06
highest = lax.Precision.HIGHEST

def rms_norm(values, norm_gain):
    inverse = lax.rsqrt(lax.optimization_barrier(jnp.mean(values * values, axis=-1, keepdims=True)) + epsilon)
    return values * inverse * norm_gain

def rope_tables(length, head_size):
    half_size = head_size // 2
    frequencies = 10000.0 ** (-(jnp.arange(half_size).astype(jnp.float32) * 2.0 / head_size))
    angles = jnp.arange(length).astype(jnp.float32)[:, None] * frequencies[None, :]
    return (jnp.cos(angles), jnp.sin(angles))

def rotate(values, cosine, sine_table):
    half_size = values.shape[-1] // 2
    first_half = values[..., :half_size]
    second = values[..., half_size:]
    cos_b = cosine[:, None, :]
    sin_b = sine_table[:, None, :]
    return jnp.concatenate([first_half * cos_b - second * sin_b, second * cos_b + first_half * sin_b], axis=-1)

def block_mask(length):
    positions = jnp.arange(length) // BLOCK
    return positions[None, :] <= positions[:, None]

def attend(queries, keys_rot, values, allowed):
    score_scale = queries.shape[-1] ** (-0.5)

    def one_head(operands):
        q_head, k_head, v_head = operands
        scores = low_back(jnp.dot(q_head, k_head.T, precision=highest) * score_scale)
        scores = jnp.where(allowed, scores, -1e+30)
        weights = low(jax.nn.softmax(scores, axis=-1))
        return jnp.dot(weights, v_head, precision=highest)
    return lax.map(jax.checkpoint(one_head), (queries, keys_rot, values))

def mixer_block(sequence, qkv_weight, out_weight, norm_gain, cosine, sine_table, allowed):
    length = sequence.shape[0]
    normed = low(rms_norm(sequence, norm_gain))
    projected = low_back(jnp.dot(normed, qkv_weight, precision=highest)).reshape(length, 3, HEADS, HEAD)
    queries = low_back(low(rotate(projected[:, 0], cosine, sine_table)))
    keys_rot = low_back(low(rotate(projected[:, 1], cosine, sine_table)))
    values = low_back(low(projected[:, 2]))
    attended = attend(queries.transpose(1, 0, 2), keys_rot.transpose(1, 0, 2), values.transpose(1, 0, 2), allowed)
    attended = low_back(low(attended.transpose(1, 0, 2).reshape(length, HEADS * HEAD)))
    return sequence + low_back(jnp.dot(attended, out_weight, precision=highest))

def placement(route_pairs, pair_order):
    pair_count = route_pairs.shape[0]
    counting = jnp.arange(pair_count).astype(jnp.int32)
    ordered = jnp.zeros((pair_count,), jnp.int32).at[pair_order].set(counting)
    sorted_ids = route_pairs[ordered]
    onehot_ids = (sorted_ids[:, None] == jnp.arange(EXPERTS + ZEROS).astype(jnp.int32)[None, :]).astype(jnp.int32)
    earlier = (jnp.cumsum(onehot_ids, axis=0) - onehot_ids).astype(jnp.int32)
    rank_sorted = lax.optimization_barrier(jnp.sum(earlier * onehot_ids, axis=1)).astype(jnp.int32)
    slot_index = rank_sorted[pair_order]
    kept_pair = (route_pairs < EXPERTS) & (slot_index < CAP)
    target = jnp.where(kept_pair, route_pairs * CAP + slot_index, EXPERTS * CAP).astype(jnp.int32)
    source = jnp.full((EXPERTS * CAP + 1,), pair_count, jnp.int32).at[target].set(counting)
    return (target, source[:EXPERTS * CAP])

def expert_apply(operands):
    rows_in, gate_w, up_w, down_w = operands
    gate_pre = low_back(jnp.dot(rows_in, gate_w, precision=highest))
    up_pre = low_back(jnp.dot(rows_in, up_w, precision=highest))
    hidden = low(gate_pre * jax.nn.sigmoid(gate_pre) * up_pre)
    return low_back(low(jnp.dot(hidden, down_w.T, precision=highest)))

def forward(tokens_f, prev_f, gain_one, qkv_f, out_f, gain_two, router_f, const_f, gate_f, up_f, down_f, route_ids, targets, sources):
    blocks = tokens_f.shape[0] // TOK_DEV
    cosine, sine_table = rope_tables(TOK_DEV, HEAD)
    allowed = block_mask(TOK_DEV)

    def one_sequence(sequence):
        return mixer_block(sequence, qkv_f, out_f, gain_one, cosine, sine_table, allowed)
    residual = lax.map(jax.checkpoint(one_sequence), tokens_f.reshape(blocks, TOK_DEV, D))
    normed = low(rms_norm(residual, gain_two))
    flat_normed = normed.reshape(-1, D)
    logits = jnp.dot(flat_normed, router_f, precision=highest) + prev_f
    chosen = jnp.take_along_axis(logits, route_ids, axis=1)
    gate_probs = jax.nn.softmax(chosen, axis=1)

    def fill_block(normed_block, source_block):
        extended = jnp.concatenate([normed_block, jnp.zeros((1, D), normed_block.dtype)], axis=0)
        token_index = jnp.where(source_block < 2 * TOK_DEV, source_block // 2, TOK_DEV).astype(jnp.int32)
        return extended[token_index]
    rows_sent = low_back(jax.vmap(fill_block)(normed, sources))
    grouped = rows_sent.reshape(blocks, EXPERTS, CAP, D).transpose(1, 0, 2, 3).reshape(EXPERTS, blocks * CAP, D)
    outputs = lax.map(jax.checkpoint(expert_apply), (grouped, gate_f, up_f, down_f))
    returned = outputs.reshape(EXPERTS, blocks, CAP, D).transpose(1, 0, 2, 3).reshape(blocks, EXPERTS * CAP, D)

    def pick_block(returned_block, target_block):
        extended = jnp.concatenate([returned_block, jnp.zeros((1, D), returned_block.dtype)], axis=0)
        return extended[target_block]
    ffn_values = jax.vmap(pick_block)(returned, targets).reshape(-1, 2, D)
    id_cube = route_ids[:, :, None]
    branch = ffn_values + jnp.where(id_cube == EXPERTS + 1, flat_normed[:, None, :], 0.0)
    branch = branch + jnp.where(id_cube == EXPERTS + 2, const_f[:, 0][None, None, :], 0.0)
    branch = branch + jnp.where(id_cube == EXPERTS + 3, const_f[:, 1][None, None, :], 0.0)
    mixture = lax.optimization_barrier(jnp.sum(gate_probs[:, :, None] * branch, axis=1))
    return residual.reshape(-1, D) + mixture

def reference(tokens, cotangent, prev_logits, routes, priority, gain_mix, mix_qkv, mix_out, gain_moe, router, constants, w_gate, w_up, w_down):
    blocks = tokens.shape[0] // TOK_DEV
    targets, sources = jax.vmap(placement)(routes.reshape(blocks, 2 * TOK_DEV), priority)
    primal = (tokens.astype(jnp.float32), prev_logits.astype(jnp.float32), gain_mix.astype(jnp.float32), mix_qkv.astype(jnp.float32), mix_out.astype(jnp.float32), gain_moe.astype(jnp.float32), router.astype(jnp.float32), constants.astype(jnp.float32), w_gate.astype(jnp.float32), w_up.astype(jnp.float32), w_down.astype(jnp.float32))

    def closed(*params):
        return forward(*params, routes, targets, sources)
    output, pullback = jax.vjp(closed, *primal)
    gradients = pullback(cotangent.astype(jnp.float32))
    return (output.astype(jnp.bfloat16), gradients[0], gradients[1], gradients[2], gradients[3], gradients[4], gradients[5], gradients[6], gradients[7], gradients[8], gradients[9], gradients[10])
```

```python
import functools

import jax
import jax.numpy as jnp
import numpy as np
from jax import lax
from jax.experimental import pallas as pl
from jax.experimental.pallas import tpu as pltpu
from jax.sharding import Mesh
from jax.sharding import PartitionSpec as P

HEADS = 12
HEAD = 64
EXPERTS = 8
ZEROS = 4
BLOCK = 256
CAP = 216
PAIRS = HEADS // 2
SLOTS = 224
GROUP = EXPERTS * SLOTS
SCALAR_ROWS = SLOTS - 16
GROUPS = ((0, 1, 2, 3), (4, 5), (6, 7))
TILE = 256
MIB = 1 << 20
LIMIT = 60
WEIGHT = 10
LIGHT = 3
LATE = 0.01
FILL = 0.01

epsilon = 1e-06
bf16 = jnp.bfloat16
f32 = jnp.float32


def dot_nn(a, b):
    return lax.dot_general(a, b, (((1,), (0,)), ((), ())), preferred_element_type=f32)


def dot_nt(a, b):
    return lax.dot_general(a, b, (((1,), (1,)), ((), ())), preferred_element_type=f32)


def dot_tn(a, b):
    return lax.dot_general(a, b, (((0,), (0,)), ((), ())), preferred_element_type=f32)


def iota(shape, axis):
    return lax.broadcasted_iota(jnp.int32, shape, axis)


def mark(condition):
    return jnp.where(condition, 1.0, 0.0).astype(bf16)


def split(value):
    high = value.astype(bf16)
    return high, (value - high.astype(f32)).astype(bf16)


def full(shape):
    return pl.BlockSpec(shape, lambda *_: (0,) * len(shape))


def rows(tile, width, steps=None):
    if steps is None:
        return pl.BlockSpec((tile, width), lambda i: (i, 0))
    return pl.BlockSpec((tile, width), lambda i: (jnp.minimum(i, steps - 1), 0))


def columns(height, tile):
    return pl.BlockSpec((height, tile), lambda i: (0, i))


SCALAR = pl.BlockSpec(memory_space=pltpu.SMEM)
WHOLE = pl.BlockSpec(memory_space=pl.ANY)


def shape(dims, dtype):
    return jax.ShapeDtypeStruct(dims, dtype)


def cost(flops, moved, weight=WEIGHT):
    return pl.CostEstimate(
        flops=int(flops * weight), bytes_accessed=int(moved * weight), transcendentals=0
    )


def params():
    return pltpu.CompilerParams(vmem_limit_bytes=LIMIT * MIB)


def nothing(*refs):
    pass


def after(value, *others):
    if not others:
        return value
    return pl.pallas_call(
        nothing,
        in_specs=[WHOLE] * (1 + len(others)),
        out_specs=WHOLE,
        out_shape=shape(value.shape, value.dtype),
        input_output_aliases={0: 0},
        name="after",
    )(value, *others)


def all_after(values, *others):
    count = len(values)
    return pl.pallas_call(
        nothing,
        in_specs=[WHOLE] * (count + len(others)),
        out_specs=[WHOLE] * count,
        out_shape=[shape(value.shape, value.dtype) for value in values],
        input_output_aliases={index: index for index in range(count)},
        name="all_after",
    )(*values, *others)


def one_hot(targets, base, count, width, axis):
    dims = (count, width) if axis == 0 else (width, count)
    slots = iota(dims, axis) + base
    first, second = targets
    return mark((slots == first) | (slots == second))


def place_body(routes_ref, order_ref, cot_ref, trow_ref, tcol_ref, piece_ref):
    length = routes_ref.shape[1]
    ids = jnp.concatenate([routes_ref[0:1, :], routes_ref[1:2, :]], axis=1)
    order = jnp.concatenate([order_ref[0:1, :], order_ref[1:2, :]], axis=1)
    high = order >> 7
    low = order & 127
    place = iota((128, 2 * length), 0)
    by_group = mark(place == ids * 16 + high)
    by_low = mark(place == low)
    table = dot_nt(by_group, by_low).astype(bf16)
    line = iota((128, 128), 0)
    lane = iota((128, 128), 1)
    before = mark(line < lane)
    groups = mark(((line >> 4) == (lane >> 4)) & ((lane & 15) < (line & 15)))
    earlier = dot_nn(groups, table).astype(bf16)
    ahead = dot_nn(table, before) + dot_nn(earlier, jnp.ones((128, 128), bf16))
    ahead = jnp.minimum(ahead, 255.0).astype(bf16)
    picked = dot_tn(ahead, by_group)
    slot = jnp.sum(jnp.where(place == low, picked, 0.0), axis=0, keepdims=True)
    slot = slot.astype(jnp.int32)
    kept = (ids < EXPERTS) & (slot < CAP)
    target = jnp.where(kept, ids * SLOTS + slot, -1)
    first = target[:, :length]
    second = target[:, length:]
    line8 = iota((8, length), 0)
    both = jnp.where(line8 == 0, first, jnp.where(line8 == 1, second, -1))
    trow_ref[...] = both
    tcol_ref[...] = jnp.transpose(both.astype(f32)).astype(jnp.int32)
    chosen = one_hot((first, second), 0, GROUP, length, 0)
    rows_out = dot_nn(chosen, cot_ref[...]).astype(bf16)
    piece_ref[...] = rows_out.reshape(EXPERTS, SLOTS, rows_out.shape[1])


def place(routes_row, order_row, cot):
    length, width = cot.shape
    dims = (EXPERTS, SLOTS, width)
    return pl.pallas_call(
        place_body,
        grid=(1,),
        in_specs=[full((2, length)), full((2, length)), full((length, width))],
        out_specs=[full((8, length)), full((length, 8)), full(dims)],
        out_shape=[
            shape((8, length), jnp.int32),
            shape((length, 8), jnp.int32),
            shape(dims, bf16),
        ],
        compiler_params=params(),
        cost_estimate=cost(2 * GROUP * length * width, 3 * length * width * 2, LIGHT),
        name="place",
    )(routes_row, order_row, cot)


def rotary(length):
    half = HEAD // 2
    frequencies = 10000.0 ** (-(np.arange(half).astype(np.float32) * 2.0 / HEAD))
    angles = np.arange(length).astype(np.float32)[:, None] * frequencies[None, :].astype(np.float32)
    cosine = np.cos(angles).astype(np.float32)
    sine = np.sin(angles).astype(np.float32)
    return (
        np.concatenate([cosine, cosine, cosine, cosine], axis=1),
        np.concatenate([-sine, sine, -sine, sine], axis=1),
    )


def turn(value, cosine, sine):
    lane = iota(value.shape, 1)
    first = (lane & (HEAD - 1)) < HEAD // 2
    other = jnp.where(
        first, pltpu.roll(value, 128 - HEAD // 2, 1), pltpu.roll(value, HEAD // 2, 1)
    )
    return value * cosine + other * sine


def project_body(starts, where_ref, tokens_ref, cos_ref, sin_ref, *rest):
    count = len(starts)
    pieces = rest[:count]
    (
        q_ref,
        k_ref,
        v_ref,
        normed_ref,
        small_ref,
        weight_out,
        out_w_out,
        weight_ref,
        out_w_ref,
        sems,
        out_sems,
    ) = rest[count:]
    back = (
        pltpu.make_async_copy(weight_ref, weight_out, out_sems.at[0]),
        pltpu.make_async_copy(out_w_ref, out_w_out, out_sems.at[1]),
    )
    width = tokens_ref.shape[1]
    wide = weight_ref.shape[1]
    step = pl.program_id(0)

    @pl.when(step == 0)
    def _():
        copies = []
        for index, piece in enumerate(pieces):
            deep = piece.shape[0]
            where = pl.ds(pl.multiple_of(where_ref[index], 16), deep)
            copies.append(
                pltpu.make_async_copy(
                    piece.at[:, :wide], weight_ref.at[where, :], sems.at[0, index]
                )
            )
            copies.append(
                pltpu.make_async_copy(
                    piece.at[:, wide:], out_w_ref.at[where, :], sems.at[1, index]
                )
            )
        for copy in copies:
            copy.start()
        for copy in copies:
            copy.wait()
        for copy in back:
            copy.start()
        extra = weight_ref[:, 3 * width :].astype(f32)
        small_ref[...] = jnp.transpose(extra)[0:16, :]

    @pl.when(step == pl.num_programs(0) - 1)
    def _():
        for copy in back:
            copy.wait()

    gain = small_ref[14:15, :]
    value = tokens_ref[...].astype(f32)
    inverse = lax.rsqrt(jnp.mean(value * value, axis=1, keepdims=True) + epsilon)
    normed = (value * inverse * gain).astype(bf16)
    normed_ref[...] = normed
    cosine = cos_ref[...]
    sine = sin_ref[...]
    for part in range(3):
        for pair in range(0, PAIRS, 2):
            start = pair * 128
            projected = dot_nn(
                normed, weight_ref[:, part * width + start : part * width + start + 256]
            )
            for half in range(2):
                cut = slice(start + half * 128, start + half * 128 + 128)
                piece = projected[:, half * 128 : half * 128 + 128]
                if part == 0:
                    q_ref[:, cut] = (turn(piece, cosine, sine).astype(bf16) * 0.125).astype(bf16)
                elif part == 1:
                    k_ref[:, cut] = turn(piece, cosine, sine).astype(bf16)
                else:
                    v_ref[:, cut] = piece.astype(bf16)


def project(tokens, pieces, where, cosine, sine):
    length, width = tokens.shape
    count = len(pieces)
    wide = pieces[0].shape[1] - width
    return pl.pallas_call(
        functools.partial(project_body, tuple(range(count))),
        grid=(length // TILE,),
        in_specs=[SCALAR, rows(TILE, width), rows(TILE, 128), rows(TILE, 128)]
        + [WHOLE] * count,
        out_specs=[rows(TILE, width)] * 4 + [full((16, width)), WHOLE, WHOLE],
        out_shape=[shape((length, width), bf16)] * 4
        + [
            shape((16, width), f32),
            shape((width, wide), bf16),
            shape((width, width), bf16),
        ],
        scratch_shapes=[
            pltpu.VMEM((width, wide), bf16),
            pltpu.VMEM((width, width), bf16),
            pltpu.SemaphoreType.DMA((2, count)),
            pltpu.SemaphoreType.DMA((2,)),
        ],
        compiler_params=params(),
        cost_estimate=cost(6 * length * width * width, 16 * length * width, LIGHT),
        name="project",
    )(where, tokens, cosine, sine, *pieces)


def attend_body(q_ref, k_ref, v_ref, out_ref, total_ref, wide_ref):
    length = q_ref.shape[0]
    wide_ref[:, :128] = v_ref[...]
    wide_ref[:, 128:] = jnp.ones((length, 128), bf16)
    lane = iota((BLOCK, 128), 1)
    for block in range(length // BLOCK):
        cut = slice(block * BLOCK, (block + 1) * BLOCK)
        seen = (block + 1) * BLOCK
        query = q_ref[cut, :]
        zero = jnp.zeros_like(query)
        result = None
        total = None
        for head in range(2):
            mine = (lane < HEAD) if head == 0 else (lane >= HEAD)
            scores = dot_nt(jnp.where(mine, query, zero), k_ref[:seen, :])
            top = jnp.max(scores, axis=1, keepdims=True)
            weights = jnp.exp(scores - top).astype(bf16)
            both = dot_nn(weights, wide_ref[:seen, :])
            summed = both[:, 128:]
            out = both[:, :128] / summed
            log_total = top + jnp.log(summed)
            if head == 0:
                result, total = out, log_total
            else:
                result = jnp.where(mine, out, result)
                total = jnp.where(mine, log_total, total)
        out_ref[cut, :] = result.astype(bf16)
        turned = jnp.transpose(total)
        total_ref[0, 0:1, cut] = turned[0:1, :]
        total_ref[0, 1:2, cut] = turned[HEAD : HEAD + 1, :]


def attend(queries, keys, values):
    length, width = queries.shape
    pair = pl.BlockSpec((length, 128), lambda i: (0, i))
    return pl.pallas_call(
        attend_body,
        grid=(PAIRS,),
        in_specs=[pair] * 3,
        out_specs=[pair, pl.BlockSpec((1, 2, length), lambda i: (i, 0, 0))],
        out_shape=[shape((length, width), bf16), shape((PAIRS, 2, length), f32)],
        scratch_shapes=[pltpu.VMEM((length, 256), bf16)],
        compiler_params=params(),
        cost_estimate=cost(8 * length * length * width, 8 * length * width, LIGHT),
        name="attend",
    )(queries, keys, values)


def mix_body(
    mine_ref,
    attended_ref,
    weight_ref,
    tokens_ref,
    cot_ref,
    small_ref,
    prev_ref,
    routes_ref,
    trow_ref,
    residual_ref,
    normed_ref,
    gates_ref,
    zero_ref,
    *rest,
):
    pieces = rest[:EXPERTS]
    kept, logits_ref, rows_all, sems = rest[EXPERTS:]
    length = kept.shape[0]
    steps = length // TILE
    step = pl.program_id(0)

    @pl.when(step < steps)
    def _():
        residual = tokens_ref[...].astype(f32) + dot_nn(attended_ref[...], weight_ref[...])
        residual_ref[...] = residual
        inverse = lax.rsqrt(jnp.mean(residual * residual, axis=1, keepdims=True) + epsilon)
        normed = (residual * inverse * small_ref[15:16, :]).astype(bf16)
        normed_ref[...] = normed
        kept[pl.ds(pl.multiple_of(step * TILE, TILE), TILE), :] = normed
        small = small_ref[...].astype(bf16)
        cot = cot_ref[...]
        high, low = split(cot.astype(f32) * normed.astype(f32))
        ones = jnp.ones((16, high.shape[1]), bf16)
        along = dot_nt(ones, high) + dot_nt(ones, low)
        constant = dot_nt(small, cot)
        line = iota((16, TILE), 0)
        where = pl.ds(pl.multiple_of(step * TILE, TILE), TILE)
        zero_ref[:, where] = jnp.where(
            line == EXPERTS + 1,
            along,
            jnp.where(
                line == EXPERTS + 2,
                constant[12:13, :],
                jnp.where(line == EXPERTS + 3, constant[13:14, :], 0.0),
            ),
        )
        logits_ref[:, where] = dot_nt(small, normed)

    @pl.when(step == steps)
    def _():
        all_ids = EXPERTS + ZEROS
        logits = logits_ref[0:all_ids, :] + prev_ref[...]
        line = iota((all_ids, length), 0)
        id0 = routes_ref[0:1, :]
        id1 = routes_ref[1:2, :]
        one = jnp.sum(jnp.where(line == id0, logits, 0.0), axis=0, keepdims=True)
        two = jnp.sum(jnp.where(line == id1, logits, 0.0), axis=0, keepdims=True)
        top = jnp.maximum(one, two)
        one = jnp.exp(one - top)
        two = jnp.exp(two - top)
        scale = 1.0 / (one + two)
        gate0 = one * scale
        gate1 = two * scale

        def gate_of(expert):
            return jnp.where(id0 == expert, gate0, jnp.where(id1 == expert, gate1, 0.0))

        line8 = iota((8, length), 0)
        gates = jnp.where(line8 == 0, gate0, jnp.where(line8 == 1, gate1, 0.0))
        for offset in range(1, ZEROS):
            expert = EXPERTS + offset
            own = jnp.where(id0 == expert, gate0, jnp.where(id1 == expert, gate1, 0.0))
            gates = jnp.where(line8 == 1 + offset, own, gates)
        gates_ref[...] = gates
        targets = (trow_ref[0:1, :], trow_ref[1:2, :])
        chosen = one_hot(targets, 0, GROUP, length, 0)
        picked = dot_nn(chosen, kept[...]).astype(bf16)
        rows_all[...] = picked.reshape(EXPERTS, SLOTS, picked.shape[1])
        line16 = iota((16, length), 0)
        expert_of = line16 & (EXPERTS - 1)
        own = jnp.where(id0 == expert_of, gate0, jnp.where(id1 == expert_of, gate1, 0.0))
        high = own.astype(bf16).astype(f32)
        both = jnp.where(line16 < EXPERTS, high, own - high)
        scalars = dot_nt(both.astype(bf16), chosen)
        for expert in range(EXPERTS):
            shift = expert * SLOTS
            turned = pltpu.roll(scalars, GROUP - shift, 1) if shift else scalars
            put_scalars(
                rows_all,
                expert,
                turned[expert : expert + 1, :TILE],
                turned[EXPERTS + expert : EXPERTS + expert + 1, :TILE],
            )
        copies = [
            pltpu.make_async_copy(rows_all.at[mine_ref[0] ^ index], piece, sems.at[index])
            for index, piece in enumerate(pieces)
        ]
        for copy in copies:
            copy.start()
        for copy in copies:
            copy.wait()


def put_scalars(target, index, high, low):
    line = iota((16, TILE), 0)
    lane = iota((16, TILE), 1)
    extra = jnp.where(line == 8, high, jnp.where(line == 9, low, 0.0))
    extra = jnp.where(lane < SLOTS, extra, 0.0)
    last = target[index, SCALAR_ROWS:, :TILE].astype(f32)
    target[index, SCALAR_ROWS:, :TILE] = (last + extra).astype(bf16)


def take_scalars(tile):
    turned = jnp.transpose(tile.astype(f32))[:SLOTS]
    return turned[:, 8:9], turned[:, 9:10]


def mix(mine, attended, weight, tokens, cot, small, prev_row, routes_row, trow):
    length, width = tokens.shape
    steps = length // TILE
    tile = rows(TILE, width, steps)
    return pl.pallas_call(
        mix_body,
        grid=(steps + 1,),
        in_specs=[
            SCALAR,
            tile,
            full(weight.shape),
            tile,
            tile,
            full(small.shape),
            full(prev_row.shape),
            full((2, length)),
            full((8, length)),
        ],
        out_specs=[tile, tile, full((8, length)), full((16, length))]
        + [WHOLE] * EXPERTS,
        out_shape=[
            shape((length, width), f32),
            shape((length, width), bf16),
            shape((8, length), f32),
            shape((16, length), f32),
        ]
        + [shape((SLOTS, width), bf16)] * EXPERTS,
        scratch_shapes=[
            pltpu.VMEM((length, width), bf16),
            pltpu.VMEM((16, length), f32),
            pltpu.VMEM((EXPERTS, SLOTS, width), bf16),
            pltpu.SemaphoreType.DMA((EXPERTS,)),
        ],
        compiler_params=params(),
        cost_estimate=cost(
            2 * length * width * width + 2 * GROUP * length * width, 18 * length * width, LIGHT),
        name="mix",
    )(mine, attended, weight, tokens, cot, small, prev_row, routes_row, trow)


def expert_body(group, chained, mine_ref, *refs):
    count = len(group)
    incoming = refs[:count]
    cot_all, weight_ref = refs[count : count + 2]
    refs = refs[count + 2 + chained :]
    hidden_ref, gate_ref, up_ref, scaled_ref, sent_ref = refs[:5]
    back = refs[5 : 5 + count]
    (
        rows_all,
        cot,
        sent,
        hidden_all,
        grads_all,
        down_all,
        in_all,
        gate_col,
        sems,
    ) = refs[5 + count :]
    step = pl.program_id(0)
    last = pl.num_programs(0) - 1
    width = rows_all.shape[1]
    part = hidden_ref.shape[1]
    inner = hidden_all.shape[1]
    deep = count * SLOTS

    @pl.when(step == 0)
    def _():
        copies = [
            pltpu.make_async_copy(cot_all.at[mine_ref[0] ^ index], cot.at[place_in], sems.at[place_in])
            for place_in, index in enumerate(group)
        ]
        for copy in copies:
            copy.start()
        for index in range(count):
            cut = slice(index * SLOTS, (index + 1) * SLOTS)
            rows_all[cut, :] = incoming[index][...]
            high, low = take_scalars(incoming[index][SCALAR_ROWS:, :TILE])
            gate_col[cut, :] = jnp.broadcast_to(high + low, (SLOTS, 128))
        for copy in copies:
            copy.wait()
        for index in range(count):
            cut = slice(index * SLOTS, (index + 1) * SLOTS)
            scaled_ref[cut, :] = (gate_col[cut, 0:1] * cot[index].astype(f32)).astype(bf16)

    value = rows_all[...]
    gate = dot_nn(value, weight_ref[0, 0])
    up = dot_nn(value, weight_ref[0, 1])
    grad_hidden = dot_nn(scaled_ref[...], weight_ref[0, 2])
    sigmoid = 1.0 / (1.0 + jnp.exp(-gate))
    active = gate * sigmoid
    hidden = (active * up).astype(bf16)
    grad_up = (grad_hidden * active).astype(bf16)
    grad_gate = (grad_hidden * up * (sigmoid + active * (1.0 - sigmoid))).astype(bf16)
    where = pl.ds(pl.multiple_of(step * part, part), part)
    behind = pl.ds(pl.multiple_of(inner + step * part, part), part)
    hidden_ref[...] = hidden
    gate_ref[...] = grad_gate
    up_ref[...] = grad_up
    hidden_all[:, where] = hidden
    grads_all[:, where] = grad_gate
    grads_all[:, behind] = grad_up
    in_all[:, where] = weight_ref[0, 0]
    in_all[:, behind] = weight_ref[0, 1]
    down_all[:, where] = weight_ref[0, 2]

    @pl.when(step == last)
    def _():
        column = gate_col[:, 0:1]
        along = None
        for start in range(0, width, TILE):
            cut = slice(start, start + TILE)
            produced = dot_nt(hidden_all[...], down_all[cut, :]).astype(bf16).astype(f32)
            sent[:, :, cut] = (produced * column).astype(bf16).reshape(count, SLOTS, TILE)
            term = jnp.sum(
                produced * cot[:, :, cut].reshape(deep, TILE).astype(f32), axis=1, keepdims=True
            )
            along = term if along is None else along + term
        copies = [
            pltpu.make_async_copy(
                sent.at[place_in], sent_ref.at[mine_ref[0] ^ index], sems.at[place_in]
            )
            for place_in, index in enumerate(group)
        ]
        for copy in copies:
            copy.start()
        for start in range(0, width, TILE):
            cut = slice(start, start + TILE)
            grads = dot_nt(grads_all[...], in_all[cut, :]).astype(bf16)
            for index in range(count):
                own = grads[index * SLOTS : (index + 1) * SLOTS]
                if start == 0:
                    scalar = along[index * SLOTS : (index + 1) * SLOTS]
                    scalar = jnp.broadcast_to(scalar, (SLOTS, 128))
                    spare = jnp.zeros((TILE - SLOTS, 128), f32)
                    scalar = jnp.transpose(jnp.concatenate([scalar, spare], axis=0))[0:16]
                    high = scalar.astype(bf16).astype(f32)
                    line = iota((16, TILE), 0)
                    extra = jnp.where(line == 8, high, jnp.where(line == 9, scalar - high, 0.0))
                    back[index][:SCALAR_ROWS, cut] = own[:SCALAR_ROWS]
                    last_rows = own[SCALAR_ROWS:].astype(f32) + extra
                    back[index][SCALAR_ROWS:, cut] = last_rows.astype(bf16)
                else:
                    back[index][:, cut] = own
        for copy in copies:
            copy.wait()


def expert_rows(group, mine, incoming, cotangents, weight, sent):
    count = len(group)
    width = incoming[0].shape[1]
    blocks, _, _, part = weight.shape
    inner = blocks * part
    deep = count * SLOTS
    chained = len(sent)
    block = pl.BlockSpec((deep, part), lambda i: (0, i))
    wide = shape((deep, inner), bf16)
    piece = full((SLOTS, width))
    return pl.pallas_call(
        functools.partial(expert_body, group, chained),
        grid=(blocks,),
        in_specs=[SCALAR]
        + [piece] * count
        + [WHOLE, pl.BlockSpec((1, 3, width, part), lambda i: (i, 0, 0, 0))]
        + [WHOLE] * chained,
        out_specs=[block, block, block, full((deep, width)), WHOLE] + [piece] * count,
        out_shape=[wide, wide, wide, shape((deep, width), bf16)]
        + [shape((EXPERTS, SLOTS, width), bf16)]
        + [shape((SLOTS, width), bf16)] * count,
        input_output_aliases={count + 3: 4} if chained else {},
        scratch_shapes=[
            pltpu.VMEM((deep, width), bf16),
            pltpu.VMEM((count, SLOTS, width), bf16),
            pltpu.VMEM((count, SLOTS, width), bf16),
            pltpu.VMEM((deep, inner), bf16),
            pltpu.VMEM((deep, 2 * inner), bf16),
            pltpu.VMEM((width, inner), bf16),
            pltpu.VMEM((width, 2 * inner), bf16),
            pltpu.VMEM((deep, 128), f32),
            pltpu.SemaphoreType.DMA((count,)),
        ],
        compiler_params=params(),
        cost_estimate=cost(12 * deep * width * inner, 6 * width * inner + 6 * deep * inner),
        name="expert_rows",
    )(mine, *incoming, cotangents, weight, *sent)


def weights_body(counts, chained, *refs):
    total = sum(counts)
    groups = len(counts)
    incoming = refs[:total]
    scaled = refs[total : total + groups]
    wide = refs[total + groups : total + 4 * groups]
    refs = refs[total + 4 * groups + chained :]
    out_ref = refs[0]
    turned = refs[1:]
    step = pl.program_id(0)

    @pl.when(step == 0)
    def _():
        start = 0
        for group, count in enumerate(counts):
            value = jnp.concatenate(
                [incoming[start + index][...] for index in range(count)], axis=0
            )
            turned[2 * group][...] = jnp.transpose(value)
            turned[2 * group + 1][...] = jnp.transpose(scaled[group][...])
            start += count

    for which in range(3):
        result = None
        for group in range(groups):
            hidden, grad_gate, grad_up = wide[3 * group : 3 * group + 3]
            left = turned[2 * group + (1 if which == 2 else 0)]
            term = dot_nn(left[...], (grad_gate, grad_up, hidden)[which][...])
            result = term if result is None else result + term
        out_ref[0, which] = result.astype(bf16)


def expert_weights(start, count, incoming, scaled, wide, blocks, made):
    width = incoming[0].shape[1]
    part = wide[0].shape[1] // blocks
    inner = count * part
    depths = [block.shape[0] for block in scaled]
    in_specs = [full((SLOTS, width))] * len(incoming)
    in_specs += [full((deep, width)) for deep in depths]
    scratch = []
    for deep in depths:
        in_specs += [pl.BlockSpec((deep, part), lambda i: (0, i + start))] * 3
        scratch += [pltpu.VMEM((width, deep), bf16)] * 2
    given = (*incoming, *scaled, *wide)
    return pl.pallas_call(
        functools.partial(weights_body, tuple(deep // SLOTS for deep in depths), len(made)),
        grid=(count,),
        in_specs=in_specs + [WHOLE] * len(made),
        out_specs=pl.BlockSpec((1, 3, width, part), lambda i: (i + start, 0, 0, 0)),
        out_shape=shape((blocks, 3, width, part), bf16),
        input_output_aliases={len(given): 0} if made else {},
        scratch_shapes=scratch,
        compiler_params=params(),
        cost_estimate=cost(
            6 * GROUP * width * inner, 6 * width * inner + 6 * GROUP * inner, FILL
        ),
        name="expert_weights",
    )(*given, *made)


def dealt(height, parts, width, split_of):
    chips, subs = split_of
    return (chips, parts, height // (chips * subs), width)


def deal(place_ref, source, keep_ref, give_ref):
    chips, parts, deep, width = keep_ref.shape
    subs = source.shape[0] // (chips * deep)
    for chip in range(chips):
        for other, target in enumerate((keep_ref, give_ref)[:subs]):
            start = ((place_ref[0] ^ chip) * subs + (place_ref[1] ^ other)) * deep
            block = source[pl.ds(pl.multiple_of(start, 16), deep), :]
            for part in range(parts):
                target[chip, part] = block[:, part * width : (part + 1) * width]


def return_body(
    place_ref,
    tcol_ref,
    routes_ref,
    gates_ref,
    zero_ref,
    small_ref,
    weight_ref,
    residual_ref,
    normed_ref,
    cot_ref,
    attended_ref,
    *rest,
):
    pieces = rest[:EXPERTS]
    logit_ref, grad_res_ref, grad_att_ref, delta_ref, keep_ref, give_ref = rest[
        EXPERTS : EXPERTS + 6
    ]
    out_sum, extra_sum, grads_all, scalars_all, back_all, sems = rest[EXPERTS + 6 :]
    step = pl.program_id(0)
    width = residual_ref.shape[1]
    id0 = routes_ref[0:1, :]
    id1 = routes_ref[1:2, :]
    line = iota((16, TILE), 0)

    @pl.when(step == 0)
    def _():
        copies = [
            pltpu.make_async_copy(piece, back_all.at[place_ref[2] ^ index], sems.at[index])
            for index, piece in enumerate(pieces)
        ]
        for copy in copies:
            copy.start()
        for copy in copies:
            copy.wait()
        lane = iota((SLOTS, 128), 1)
        for expert in range(EXPERTS):
            high, low = take_scalars(back_all[expert, SCALAR_ROWS:, :TILE])
            spot = jnp.where(lane == expert, high, jnp.where(lane == EXPERTS + expert, low, 0.0))
            scalars_all[expert * SLOTS : (expert + 1) * SLOTS, :] = spot.astype(bf16)

    chosen = one_hot((tcol_ref[:, 0:1], tcol_ref[:, 1:2]), 0, GROUP, TILE, 1)
    from_rows = dot_nn(chosen, back_all[...].reshape(GROUP, width))
    scalars = jnp.transpose(dot_nn(chosen, scalars_all[...]))
    through = jnp.concatenate(
        [scalars[:EXPERTS] + scalars[EXPERTS : 2 * EXPERTS], zero_ref[EXPERTS:]], axis=0
    )
    gate0 = gates_ref[0:1, :]
    gate1 = gates_ref[1:2, :]
    grad0 = jnp.sum(jnp.where(line == id0, through, 0.0), axis=0, keepdims=True)
    grad1 = jnp.sum(jnp.where(line == id1, through, 0.0), axis=0, keepdims=True)
    mean = gate0 * grad0 + gate1 * grad1
    chosen0 = gate0 * (grad0 - mean)
    chosen1 = gate1 * (grad1 - mean)
    logit = jnp.where(line == id0, chosen0, jnp.where(line == id1, chosen1, 0.0))
    logit_ref[...] = logit[: EXPERTS + ZEROS]
    logit_high, logit_low = split(logit)
    small = small_ref[...].astype(bf16)
    both = jnp.concatenate([logit_high.astype(f32), logit_low.astype(f32)], axis=0).astype(bf16)
    twice = jnp.concatenate([small_ref[...], small_ref[...]], axis=0).astype(bf16)
    grad_normed = dot_tn(both, twice)
    grad_normed += from_rows
    cot = cot_ref[...]
    cot_wide = cot.astype(f32)
    gate_cols = jnp.transpose(gates_ref[...])
    grad_normed += gate_cols[:, 2:3] * cot_wide
    residual = residual_ref[...]
    gain = small_ref[15:16, :]
    inverse = lax.rsqrt(jnp.mean(residual * residual, axis=1, keepdims=True) + epsilon)
    scaled = grad_normed * gain
    spread = jnp.mean(scaled * residual, axis=1, keepdims=True)
    grad_residual = cot_wide + inverse * scaled - residual * (inverse * inverse * inverse * spread)
    grad_res_ref[...] = grad_residual
    grad_low = grad_residual.astype(bf16)
    grad_att = dot_nt(grad_low, weight_ref[...]).astype(bf16)
    grad_att_ref[...] = grad_att
    attended = attended_ref[...]
    product = (grad_att.astype(f32) * attended.astype(f32)).astype(bf16)
    head_of = (iota((16, width), 1) >> 6) == iota((16, width), 0)
    delta = dot_nt(mark(head_of), product)
    for pair in range(PAIRS):
        delta_ref[pair] = delta[2 * pair : 2 * pair + 2, :]
    out_term = dot_tn(attended, grad_low)
    grad_gain = jnp.sum(grad_normed * residual * inverse, axis=0, keepdims=True)
    normed = normed_ref[...]
    router_term = dot_nn(logit_high, normed) + dot_nn(logit_low, normed)
    const0 = gates_ref[3:4, :]
    const1 = gates_ref[4:5, :]
    weights = jnp.where(line == 12, const0, jnp.where(line == 13, const1, 0.0))
    const_high, const_low = split(weights)
    const_term = dot_nn(const_high, cot) + dot_nn(const_low, cot)
    extra = router_term + const_term
    extra = jnp.where(iota((16, width), 0) == 15, grad_gain, extra)

    @pl.when(step == 0)
    def _():
        out_sum[...] = out_term
        extra_sum[...] = jnp.zeros_like(extra_sum)
        extra_sum[0:16, :] = extra

    @pl.when(step > 0)
    def _():
        out_sum[...] += out_term
        extra_sum[0:16, :] += extra

    @pl.when(step == pl.num_programs(0) - 1)
    def _():
        small_grads = jnp.transpose(extra_sum[...]).astype(bf16)
        grads_all[:, :width] = out_sum[...].astype(bf16)
        grads_all[:, width:] = small_grads
        deal(place_ref, grads_all, keep_ref, give_ref)


def come_back(
    place_of,
    tcol,
    routes_row,
    gates,
    zero,
    small,
    weight,
    residual,
    normed,
    cot,
    attended,
    pieces,
    split_of,
):
    length, width = cot.shape
    steps = length // TILE
    tile = rows(TILE, width)
    dims = dealt(width, 1, width + 128, split_of)
    all_ids = EXPERTS + ZEROS
    return pl.pallas_call(
        return_body,
        grid=(steps,),
        in_specs=[
            SCALAR,
            rows(TILE, 8),
            columns(2, TILE),
            columns(8, TILE),
            columns(16, TILE),
            full(small.shape),
            full(weight.shape),
            tile,
            tile,
            tile,
            tile,
        ]
        + [WHOLE] * EXPERTS,
        out_specs=[
            columns(all_ids, TILE),
            tile,
            tile,
            pl.BlockSpec((PAIRS, 2, TILE), lambda i: (0, 0, i)),
            full(dims),
            full(dims),
        ],
        out_shape=[
            shape((all_ids, length), f32),
            shape((length, width), f32),
            shape((length, width), bf16),
            shape((PAIRS, 2, length), f32),
            shape(dims, bf16),
            shape(dims, bf16),
        ],
        scratch_shapes=[
            pltpu.VMEM((width, width), f32),
            pltpu.VMEM((128, width), f32),
            pltpu.VMEM((width, width + 128), bf16),
            pltpu.VMEM((GROUP, 128), bf16),
            pltpu.VMEM((EXPERTS, SLOTS, width), bf16),
            pltpu.SemaphoreType.DMA((EXPERTS,)),
        ],
        compiler_params=params(),
        cost_estimate=cost(
            4 * length * width * width + 2 * GROUP * length * width, 18 * length * width, 30),
        name="come_back",
    )(
        place_of,
        tcol,
        routes_row,
        gates,
        zero,
        small,
        weight,
        residual,
        normed,
        cot,
        attended,
        *pieces,
    )


def attend_back_body(
    place_ref,
    q_ref,
    k_ref,
    v_ref,
    grad_ref,
    total_ref,
    delta_ref,
    cos_ref,
    sin_ref,
    normed_ref,
    grads_ref,
    keep_ref,
    give_ref,
    turned,
    normed_turned,
    weight_grads,
):
    @pl.when(pl.program_id(0) == 0)
    def _():
        normed_turned[...] = jnp.transpose(normed_ref[...])

    length = q_ref.shape[0]
    cosine = cos_ref[...]
    sine = sin_ref[...]
    lane = iota((BLOCK, 128), 1)
    keys_turned = jnp.transpose(k_ref[...])
    line = iota((128, BLOCK), 0)
    for block in range(length // BLOCK):
        start = block * BLOCK
        cut = slice(start, start + BLOCK)
        key = k_ref[cut, :]
        value = v_ref[cut, :]
        zero = jnp.zeros_like(key)
        query = q_ref[start:, :]
        grad = grad_ref[start:, :]
        grad_key = None
        grad_value = None
        for head in range(2):
            mine = (lane < HEAD) if head == 0 else (lane >= HEAD)
            scores = dot_nt(jnp.where(mine, key, zero), query)
            weights = jnp.exp(scores - total_ref[0, head : head + 1, start:])
            grad_weights = dot_nt(jnp.where(mine, value, zero), grad)
            grad_scores = weights * (grad_weights - delta_ref[0, head : head + 1, start:])
            grad_scores = grad_scores.astype(bf16)
            value_term = dot_nn(weights.astype(bf16), grad)
            key_term = dot_nn(grad_scores, query)
            key_mine = (line < HEAD) if head == 0 else (line >= HEAD)
            key_line = keys_turned[:, cut]
            query_term = dot_nn(jnp.where(key_mine, key_line, jnp.zeros_like(key_line)), grad_scores)
            if block == 0 and head == 0:
                turned[...] = query_term
            else:
                turned[:, start:] += query_term
            if head == 0:
                grad_key, grad_value = key_term, value_term
            else:
                grad_key = jnp.where(mine, key_term, grad_key)
                grad_value = jnp.where(mine, value_term, grad_value)
        grad_key = grad_key.astype(bf16).astype(f32)
        grads_ref[cut, 128:256] = turn(grad_key, cosine[cut], -sine[cut]).astype(bf16)
        grads_ref[cut, 256:] = grad_value.astype(bf16)
    grad_query = (jnp.transpose(turned[...]) * 0.125).astype(bf16).astype(f32)
    grads_ref[:, :128] = turn(grad_query, cosine, -sine).astype(bf16)
    weight_grads[...] = dot_nn(normed_turned[...], grads_ref[...]).astype(bf16)
    deal(place_ref, weight_grads, keep_ref, give_ref)


def attend_back(
    first, count, place_of, queries, keys, values, grad, total, delta, cosine, sine, normed, split_of
):
    length, width = queries.shape
    pair = pl.BlockSpec((length, 128), lambda i: (0, i + first))
    line = pl.BlockSpec((1, 2, length), lambda i: (i + first, 0, 0))
    chips, parts, deep, across = dealt(width, 3, 128 * count, split_of)
    block = pl.BlockSpec((chips, parts, deep, 128), lambda i: (0, 0, 0, i))
    dims = shape((chips, parts, deep, across), bf16)
    return pl.pallas_call(
        attend_back_body,
        grid=(count,),
        in_specs=[SCALAR]
        + [pair] * 4
        + [line, line, full((length, 128)), full((length, 128)), full((length, width))],
        out_specs=[columns(length, 384), block, block],
        out_shape=[shape((length, 384 * count), bf16), dims, dims],
        scratch_shapes=[
            pltpu.VMEM((128, length), f32),
            pltpu.VMEM((width, length), bf16),
            pltpu.VMEM((width, 384), bf16),
        ],
        compiler_params=params(),
        cost_estimate=cost(
            26 * length * length * 128 * count, 14 * length * 128 * count, LATE),
        name="attend_back",
    )(place_of, queries, keys, values, grad, total, delta, cosine, sine, normed)


def tokens_grad_body(first_ref, second_ref, weight_ref, tokens_ref, grad_res_ref, small_ref, out_ref):
    width = tokens_ref.shape[1]
    grad_normed = None
    for group, ref in enumerate((first_ref, second_ref)):
        pairs = ref.shape[1] // 384
        for part in range(3):
            start = part * width + group * pairs * 128
            grads = jnp.concatenate(
                [
                    ref[:, pair * 384 + part * 128 : pair * 384 + part * 128 + 128]
                    for pair in range(pairs)
                ],
                axis=1,
            )
            term = dot_nt(grads, weight_ref[:, start : start + pairs * 128])
            grad_normed = term if grad_normed is None else grad_normed + term
    value = tokens_ref[...].astype(f32)
    inverse = lax.rsqrt(jnp.mean(value * value, axis=1, keepdims=True) + epsilon)
    scaled = grad_normed * small_ref[14:15, :]
    spread_of = jnp.mean(scaled * value, axis=1, keepdims=True)
    grad = inverse * scaled - value * (inverse * inverse * inverse * spread_of)
    out_ref[...] = grad_res_ref[...] + grad


def tokens_grad(grads, weight, tokens, grad_res, small):
    length, width = tokens.shape
    tile = rows(TILE, width)
    wide = grads[0].shape[1]
    return pl.pallas_call(
        tokens_grad_body,
        grid=(length // TILE,),
        in_specs=[rows(TILE, wide)] * 2
        + [full(weight.shape), tile, tile, full(small.shape)],
        out_specs=tile,
        out_shape=shape((length, width), f32),
        compiler_params=params(),
        cost_estimate=cost(6 * length * width * width, 16 * length * width, LATE),
        name="tokens_grad",
    )(*grads, weight, tokens, grad_res, small)


def output_body(
    tcol_ref, gates_ref, small_ref, residual_ref, normed_ref, block_ref, out_ref
):
    gates = gates_ref[...]
    line = iota(gates.shape, 0)
    gate_cols = jnp.transpose(gates)
    consts = jnp.where((line == 3) | (line == 4), gates, 0.0)
    high, low = split(consts)
    vectors = jnp.where(iota((8, small_ref.shape[1]), 0) == 3, small_ref[12:13, :], 0.0)
    vectors = jnp.where(
        iota((8, small_ref.shape[1]), 0) == 4, small_ref[13:14, :], vectors
    )
    both = jnp.concatenate([high.astype(f32), low.astype(f32)], axis=0).astype(bf16)
    twice = jnp.concatenate([vectors, vectors], axis=0).astype(bf16)
    total = residual_ref[...] + dot_tn(both, twice)
    total += gate_cols[:, 2:3] * normed_ref[...].astype(f32)
    chosen = one_hot((tcol_ref[:, 0:1], tcol_ref[:, 1:2]), 0, GROUP, TILE, 1)
    total += dot_nn(chosen, block_ref[...].reshape(GROUP, block_ref.shape[2]))
    out_ref[...] = total.astype(bf16)


def output(tcol, gates, small, residual, normed, block):
    length, width = residual.shape
    tile = rows(TILE, width)
    return pl.pallas_call(
        output_body,
        grid=(length // TILE,),
        in_specs=[rows(TILE, 8), columns(8, TILE), full(small.shape), tile, tile]
        + [full((EXPERTS, SLOTS, width))],
        out_specs=tile,
        out_shape=shape((length, width), bf16),
        compiler_params=params(),
        cost_estimate=cost(2 * GROUP * length * width, 12 * length * width, LATE),
        name="output",
    )(tcol, gates, small, residual, normed, block)


def local(
    tokens,
    cotangent,
    prev_logits,
    routes,
    priority,
    gain_mix,
    mix_qkv,
    mix_out,
    gain_moe,
    router,
    constants,
    w_gate,
    w_up,
    w_down,
):
    length, width = tokens.shape
    here, _, part = w_gate.shape
    depth = lax.axis_size("expert")
    chips = lax.axis_size("chip")
    z = lax.axis_index("expert").astype(jnp.int32)
    chip = lax.axis_index("chip").astype(jnp.int32)
    sub = lax.axis_index("sub").astype(jnp.int32)
    pairwise = chips == 4 and here == 2
    split_of = (chips, here) if pairwise else (1, 1)
    own = (z * here + sub).astype(jnp.int32)
    mine_of = own.reshape(1)
    spot = (chip, sub) if pairwise else (jnp.int32(0), jnp.int32(0))
    place_of = jnp.stack([*spot, own])
    members = [(a, b) for a in range(depth) for b in range(here)]

    def partner(index, value):
        if index == 0:
            return value
        moves = []
        for source, (a, b) in enumerate(members):
            c, d = members[source ^ index]
            moves += [
                ((a * chips + i) * here + b, (c * chips + i) * here + d) for i in range(chips)
            ]
        return lax.ppermute(value, ("expert", "chip", "sub"), moves)

    def trade(value, axis, size, index):
        return lax.ppermute(value, axis, [(i, i ^ index) for i in range(size)])

    def exchange(value):
        return lax.all_to_all(value, ("expert", "sub"), split_axis=0, concat_axis=0, tiled=True)

    features = mix_qkv.shape[0]
    extra = jnp.concatenate(
        [router, constants, gain_mix[:, None], gain_moe[:, None]], axis=1
    )
    extra = jnp.pad(extra, ((0, 0), (0, 128 - extra.shape[1])))
    packed = jnp.concatenate([mix_qkv, extra, mix_out], axis=1)
    routes_row = routes.T
    order_row = priority.reshape(length, 2).T
    trow, tcol, grads_out = place(routes_row, order_row, cotangent)
    cot_in = exchange(grads_out)

    if pairwise:
        near = [trade(packed, "chip", chips, index) for index in (1, 2)]
    else:
        near = [packed]

    def of_expert(index):
        return jnp.stack(
            [lax.dynamic_index_in_dim(w, index, 0, keepdims=False) for w in (w_gate, w_up, w_down)]
        )

    keep = of_expert(sub)
    if here == 1:
        mine = keep[None]
    else:
        give = of_expert(1 - sub)
        mine = jnp.stack([keep, trade(give, "sub", here, 1)], axis=0)
    weight = lax.all_gather(mine, "chip", axis=0, tiled=True)
    count = weight.shape[0]
    if part < 256:
        join = 256 // part
        weight = weight.reshape(count // join, join, 3, width, part)
        weight = weight.transpose(0, 2, 3, 1, 4).reshape(count // join, 3, width, 256)

    if pairwise:
        near = [after(piece, trow, mine) for piece in near]
        half = features // 2
        far = [
            trade(near[1][:half], "chip", chips, 1),
            trade(near[0][half:], "chip", chips, 2),
        ]
        pieces = [packed, *near, *far]
        spots = [chip, chip ^ 1, chip ^ 2, chip ^ 3, chip ^ 3]
        lower = [0, 0, 0, 0, half]
        pieces += [trade(piece, "sub", here, 1) for piece in pieces]
        where = jnp.stack(
            [(spot * here + sub) * features + low for spot, low in zip(spots, lower)]
            + [(spot * here + (sub ^ 1)) * features + low for spot, low in zip(spots, lower)]
        )
    else:
        pieces = [lax.all_gather(packed, ("chip", "sub"), axis=0, tiled=True)]
        where = jnp.zeros((1,), jnp.int32)

    cosine, sine = rotary(length)
    outs = project(tokens, pieces, where, cosine, sine)
    queries, keys, values, normed_one, small, qkv, out_w = outs
    attended, log_total = attend(queries, keys, values)
    outs = mix(mine_of, attended, out_w, tokens, cotangent, small, prev_logits.T, routes_row, trow)
    residual, normed_two, gates, zero = outs[:4]
    leaving = outs[4:]
    rows_in = [None] * EXPERTS
    returned = [None] * EXPERTS
    near = GROUPS[0][1:]
    far = [index for group in GROUPS[1:] for index in group]
    for index in GROUPS[0]:
        rows_in[index] = partner(index, leaving[index])
    crossing = all_after([leaving[index] for index in far], *[rows_in[index] for index in near])
    for index, block in zip(far, crossing):
        rows_in[index] = partner(index, block)

    sent, scaled, wide, ordered = [], [], [], []
    blocks = weight.shape[0]
    for group in GROUPS[:2]:
        incoming = [rows_in[index] for index in group]
        outs = expert_rows(group, mine_of, incoming, cot_in, weight, sent)
        wide += outs[:3]
        scaled.append(outs[3])
        sent = [outs[4]]
        ordered += incoming
        for index, block in zip(group, outs[5:]):
            returned[index] = partner(index, block)
    group = GROUPS[2]
    incoming = [rows_in[index] for index in group]
    sent[0] = after(sent[0], *[returned[index] for index in near])
    outs = expert_rows(group, mine_of, incoming, cot_in, weight, sent)
    wide += outs[:3]
    scaled.append(outs[3])
    sent = outs[4]
    ordered += incoming
    early = 3 * blocks // 8
    grads_w = [expert_weights(0, early, ordered, scaled, wide, blocks, [])]
    before = [returned[index] for index in GROUPS[1]] + grads_w
    for index, block in zip(group, all_after(outs[5:], *before)):
        returned[index] = partner(index, block)
    grads_w = expert_weights(
        early, blocks - early, ordered, scaled, wide, blocks, grads_w
    )
    residual_late = after(residual, grads_w)
    produced = exchange(sent)

    if part < 256:
        grads_w = grads_w.reshape(count // join, 3, width, join, part)
        grads_w = grads_w.transpose(0, 3, 1, 2, 4).reshape(count, 3, width, part)
    grads_w = lax.psum_scatter(grads_w, "chip", scatter_dimension=0, tiled=True)
    outs = come_back(
        place_of,
        tcol,
        routes_row,
        gates,
        zero,
        small,
        out_w,
        residual_late,
        normed_two,
        cotangent,
        attended,
        returned,
        split_of,
    )
    logit_grad, grad_res, grad_att, delta = outs[:4]
    dealt_out = outs[4:]

    def flat(block):
        return block.transpose(1, 0, 2).reshape(block.shape[1], -1)

    def over_cores(dealt_parts):
        if not pairwise:
            return [jnp.concatenate([flat(keep[0]) for keep, _ in dealt_parts], axis=1)]
        got = [trade(give, "sub", here, 1) for _, give in dealt_parts]
        sums = []
        for index in range(chips):
            both = [
                flat(keep[index]).astype(f32) + flat(other[index]).astype(f32)
                for (keep, _), other in zip(dealt_parts, got)
            ]
            sums.append(jnp.concatenate(both, axis=1).astype(bf16 if index else f32))
        return sums

    def over_chips(sums):
        if not pairwise:
            axes = ("chip", "sub")
            return lax.psum_scatter(sums[0], axes, scatter_dimension=0, tiled=True).astype(f32)
        total = sums[0]
        for index in range(1, chips):
            total += trade(sums[index], "chip", chips, index).astype(f32)
        return total

    def over_planes(total, index):
        low = total.astype(bf16)
        return low.astype(f32) + trade(low, "expert", depth, index).astype(f32)

    def back_through(first, normed):
        return attend_back(
            first,
            count,
            place_of,
            queries,
            keys,
            values,
            grad_att,
            log_total,
            delta,
            cosine,
            sine,
            normed,
            split_of,
        )

    count = PAIRS // 2
    grads_a, *dealt_a = back_through(0, normed_one)
    sums_a = over_cores([dealt_a, dealt_out])
    grads_b, *dealt_b = back_through(count, after(normed_one, sums_a[-1]))
    total_a = over_chips([after(sums_a[0], grads_b), *sums_a[1:]])
    dealt_b[0] = after(dealt_b[0], produced)
    sums_b = over_cores([dealt_b])
    total_a = after(over_planes(total_a, 1), sums_b[-1])
    token_grad = tokens_grad([grads_a, grads_b], qkv, tokens, after(grad_res, total_a), small)
    total_b = over_chips([after(sums_b[0], token_grad), *sums_b[1:]])
    block_out = output(tcol, gates, small, after(residual, total_b), normed_two, produced)
    index = 2
    while index < depth:
        total_a = over_planes(total_a, index)
        index *= 2
    index = 1
    while index < depth:
        total_b = over_planes(total_b, index)
        index *= 2
    summed = [total_a, total_b]

    if here == 1:
        grads_w = grads_w[0][:, None].astype(f32)
    else:
        own = grads_w[0]
        theirs = trade(after(grads_w[1], block_out), "sub", here, 1)
        pair = jnp.stack([own, theirs], axis=1).astype(f32)
        swapped = jnp.stack([theirs, own], axis=1).astype(f32)
        grads_w = jnp.where(sub == 0, pair, swapped)

    across = 128 * count
    mixed = summed[0][:, 3 * across :]
    grad_qkv = jnp.concatenate(
        [
            part[:, index * across : (index + 1) * across]
            for index in range(3)
            for part in summed
        ],
        axis=1,
    )
    grad_gain = jnp.sum(grad_qkv * mix_qkv.astype(f32), axis=1) / gain_mix.astype(f32)
    all_ids = EXPERTS + ZEROS
    return (
        block_out,
        token_grad,
        logit_grad.T,
        grad_gain,
        grad_qkv,
        mixed[:, :width],
        mixed[:, width + 15],
        mixed[:, width : width + all_ids],
        mixed[:, width + 12 : width + 14],
        grads_w[0],
        grads_w[1],
        grads_w[2],
    )


def solution(mesh):
    depth = mesh.shape["expert"]
    here = EXPERTS // depth
    chips = mesh.shape["shard"] // here
    fine = Mesh(mesh.devices.reshape(depth, chips, here), ("expert", "chip", "sub"))
    shard = ("chip", "sub")
    by_token = P(("expert", "chip", "sub"), None)
    weights = P("expert", None, shard)
    mixer = (P(shard), P(shard, None), P(shard, None), P(shard), P(shard, None), P(shard, None))
    in_specs = (by_token,) * 5 + mixer + (weights,) * 3
    out_specs = (by_token,) * 3 + mixer + (weights,) * 3
    return jax.shard_map(
        local, mesh=fine, in_specs=in_specs, out_specs=out_specs, check_vma=False
    )
```

```python
import functools

import jax
import jax.numpy as jnp
import numpy as np
from jax import lax
from jax.experimental import pallas as pl
from jax.experimental.pallas import tpu as pltpu
from jax.sharding import Mesh
from jax.sharding import PartitionSpec as P

HEADS = 12
HEAD = 64
EXPERTS = 8
ZEROS = 4
BLOCK = 256
CAP = 216
PAIRS = HEADS // 2
SLOTS = 224
GROUP = EXPERTS * SLOTS
SCALAR_ROWS = SLOTS - 16
GROUPS = ((0, 1, 2, 3), (4, 5), (6, 7))
TILE = 256
ROWS = 512
MIB = 1 << 20
LIMIT = 60
WEIGHT = 10
LIGHT = 2.6
LATE = 0.01
FILL = 0.01

epsilon = 1e-06
bf16 = jnp.bfloat16
f32 = jnp.float32


def dot_nn(a, b):
    return lax.dot_general(a, b, (((1,), (0,)), ((), ())), preferred_element_type=f32)


def dot_nt(a, b):
    return lax.dot_general(a, b, (((1,), (1,)), ((), ())), preferred_element_type=f32)


def dot_tn(a, b):
    return lax.dot_general(a, b, (((0,), (0,)), ((), ())), preferred_element_type=f32)


def iota(shape, axis):
    return lax.broadcasted_iota(jnp.int32, shape, axis)


def mark(condition):
    return jnp.where(condition, 1.0, 0.0).astype(bf16)


def split(value):
    high = value.astype(bf16)
    return high, (value - high.astype(f32)).astype(bf16)


def full(shape):
    return pl.BlockSpec(shape, lambda *_: (0,) * len(shape))


def rows(tile, width, steps=None):
    if steps is None:
        return pl.BlockSpec((tile, width), lambda i: (i, 0))
    return pl.BlockSpec((tile, width), lambda i: (jnp.minimum(i, steps - 1), 0))


def columns(height, tile):
    return pl.BlockSpec((height, tile), lambda i: (0, i))


SCALAR = pl.BlockSpec(memory_space=pltpu.SMEM)
WHOLE = pl.BlockSpec(memory_space=pl.ANY)


def shape(dims, dtype):
    return jax.ShapeDtypeStruct(dims, dtype)


def cost(flops, moved, weight=WEIGHT):
    return pl.CostEstimate(
        flops=int(flops * weight), bytes_accessed=int(moved * weight), transcendentals=0
    )


def params():
    return pltpu.CompilerParams(vmem_limit_bytes=LIMIT * MIB)


def nothing(*refs):
    pass


def after(value, *others):
    if not others:
        return value
    return pl.pallas_call(
        nothing,
        in_specs=[WHOLE] * (1 + len(others)),
        out_specs=WHOLE,
        out_shape=shape(value.shape, value.dtype),
        input_output_aliases={0: 0},
        name="after",
    )(value, *others)


def all_after(values, *others):
    count = len(values)
    return pl.pallas_call(
        nothing,
        in_specs=[WHOLE] * (count + len(others)),
        out_specs=[WHOLE] * count,
        out_shape=[shape(value.shape, value.dtype) for value in values],
        input_output_aliases={index: index for index in range(count)},
        name="all_after",
    )(*values, *others)


def one_hot(targets, base, count, width, axis):
    dims = (count, width) if axis == 0 else (width, count)
    slots = iota(dims, axis) + base
    first, second = targets
    return mark((slots == first) | (slots == second))


def place_body(routes_ref, order_ref, cot_ref, trow_ref, tcol_ref, piece_ref):
    length = routes_ref.shape[1]
    ids = jnp.concatenate([routes_ref[0:1, :], routes_ref[1:2, :]], axis=1)
    order = jnp.concatenate([order_ref[0:1, :], order_ref[1:2, :]], axis=1)
    high = order >> 7
    low = order & 127
    place = iota((128, 2 * length), 0)
    by_group = mark(place == ids * 16 + high)
    by_low = mark(place == low)
    table = dot_nt(by_group, by_low).astype(bf16)
    line = iota((128, 128), 0)
    lane = iota((128, 128), 1)
    before = mark(line < lane)
    groups = mark(((line >> 4) == (lane >> 4)) & ((lane & 15) < (line & 15)))
    earlier = dot_nn(groups, table).astype(bf16)
    ahead = dot_nn(table, before) + dot_nn(earlier, jnp.ones((128, 128), bf16))
    ahead = jnp.minimum(ahead, 255.0).astype(bf16)
    picked = dot_tn(ahead, by_group)
    slot = jnp.sum(jnp.where(place == low, picked, 0.0), axis=0, keepdims=True)
    slot = slot.astype(jnp.int32)
    kept = (ids < EXPERTS) & (slot < CAP)
    target = jnp.where(kept, ids * SLOTS + slot, -1)
    first = target[:, :length]
    second = target[:, length:]
    line8 = iota((8, length), 0)
    both = jnp.where(line8 == 0, first, jnp.where(line8 == 1, second, -1))
    trow_ref[...] = both
    tcol_ref[...] = jnp.transpose(both.astype(f32)).astype(jnp.int32)
    chosen = one_hot((first, second), 0, GROUP, length, 0)
    rows_out = dot_nn(chosen, cot_ref[...]).astype(bf16)
    piece_ref[...] = rows_out.reshape(EXPERTS, SLOTS, rows_out.shape[1])


def place(routes_row, order_row, cot):
    length, width = cot.shape
    dims = (EXPERTS, SLOTS, width)
    return pl.pallas_call(
        place_body,
        grid=(1,),
        in_specs=[full((2, length)), full((2, length)), full((length, width))],
        out_specs=[full((8, length)), full((length, 8)), full(dims)],
        out_shape=[
            shape((8, length), jnp.int32),
            shape((length, 8), jnp.int32),
            shape(dims, bf16),
        ],
        compiler_params=params(),
        cost_estimate=cost(2 * GROUP * length * width, 3 * length * width * 2, LIGHT),
        name="place",
    )(routes_row, order_row, cot)


def rotary(length):
    half = HEAD // 2
    frequencies = 10000.0 ** (-(np.arange(half).astype(np.float32) * 2.0 / HEAD))
    angles = np.arange(length).astype(np.float32)[:, None] * frequencies[None, :].astype(np.float32)
    cosine = np.cos(angles).astype(np.float32)
    sine = np.sin(angles).astype(np.float32)
    return (
        np.concatenate([cosine, cosine, cosine, cosine], axis=1),
        np.concatenate([-sine, sine, -sine, sine], axis=1),
    )


def turn(value, cosine, sine):
    lane = iota(value.shape, 1)
    first = (lane & (HEAD - 1)) < HEAD // 2
    other = jnp.where(
        first, pltpu.roll(value, 128 - HEAD // 2, 1), pltpu.roll(value, HEAD // 2, 1)
    )
    return value * cosine + other * sine


def project_body(starts, where_ref, tokens_ref, cos_ref, sin_ref, *rest):
    count = len(starts)
    pieces = rest[:count]
    (
        q_ref,
        k_ref,
        v_ref,
        normed_ref,
        small_ref,
        weight_out,
        out_w_out,
        weight_ref,
        out_w_ref,
        sems,
        out_sems,
    ) = rest[count:]
    back = (
        pltpu.make_async_copy(weight_ref, weight_out, out_sems.at[0]),
        pltpu.make_async_copy(out_w_ref, out_w_out, out_sems.at[1]),
    )
    width = tokens_ref.shape[1]
    wide = weight_ref.shape[1]
    step = pl.program_id(0)

    @pl.when(step == 0)
    def _():
        copies = []
        for index, piece in enumerate(pieces):
            deep = piece.shape[0]
            where = pl.ds(pl.multiple_of(where_ref[index], 16), deep)
            copies.append(
                pltpu.make_async_copy(
                    piece.at[:, :wide], weight_ref.at[where, :], sems.at[0, index]
                )
            )
            copies.append(
                pltpu.make_async_copy(
                    piece.at[:, wide:], out_w_ref.at[where, :], sems.at[1, index]
                )
            )
        for copy in copies:
            copy.start()
        for copy in copies:
            copy.wait()
        for copy in back:
            copy.start()
        extra = weight_ref[:, 3 * width :].astype(f32)
        small_ref[...] = jnp.transpose(extra)[0:16, :]

    @pl.when(step == pl.num_programs(0) - 1)
    def _():
        for copy in back:
            copy.wait()

    gain = small_ref[14:15, :]
    value = tokens_ref[...].astype(f32)
    inverse = lax.rsqrt(jnp.mean(value * value, axis=1, keepdims=True) + epsilon)
    normed = (value * inverse * gain).astype(bf16)
    normed_ref[...] = normed
    cosine = cos_ref[...]
    sine = sin_ref[...]
    for part in range(3):
        for pair in range(0, PAIRS, 2):
            start = pair * 128
            projected = dot_nn(
                normed, weight_ref[:, part * width + start : part * width + start + 256]
            )
            for half in range(2):
                cut = slice(start + half * 128, start + half * 128 + 128)
                piece = projected[:, half * 128 : half * 128 + 128]
                if part == 0:
                    q_ref[:, cut] = (turn(piece, cosine, sine).astype(bf16) * 0.125).astype(bf16)
                elif part == 1:
                    k_ref[:, cut] = turn(piece, cosine, sine).astype(bf16)
                else:
                    v_ref[:, cut] = piece.astype(bf16)


def project(tokens, pieces, where, cosine, sine):
    length, width = tokens.shape
    count = len(pieces)
    wide = pieces[0].shape[1] - width
    return pl.pallas_call(
        functools.partial(project_body, tuple(range(count))),
        grid=(length // ROWS,),
        in_specs=[SCALAR, rows(ROWS, width), rows(ROWS, 128), rows(ROWS, 128)]
        + [WHOLE] * count,
        out_specs=[rows(ROWS, width)] * 4 + [full((16, width)), WHOLE, WHOLE],
        out_shape=[shape((length, width), bf16)] * 4
        + [
            shape((16, width), f32),
            shape((width, wide), bf16),
            shape((width, width), bf16),
        ],
        scratch_shapes=[
            pltpu.VMEM((width, wide), bf16),
            pltpu.VMEM((width, width), bf16),
            pltpu.SemaphoreType.DMA((2, count)),
            pltpu.SemaphoreType.DMA((2,)),
        ],
        compiler_params=params(),
        cost_estimate=cost(6 * length * width * width, 16 * length * width, LIGHT),
        name="project",
    )(where, tokens, cosine, sine, *pieces)


def attend_body(q_ref, k_ref, v_ref, out_ref, total_ref, wide_ref):
    length = q_ref.shape[0]
    wide_ref[:, :128] = v_ref[...]
    wide_ref[:, 128:] = jnp.ones((length, 128), bf16)
    lane = iota((BLOCK, 128), 1)

    def score(block, head):
        mine = (lane < HEAD) if head == 0 else (lane >= HEAD)
        query = q_ref[block * BLOCK : (block + 1) * BLOCK, :]
        query = jnp.where(mine, query, jnp.zeros_like(query))
        return dot_nt(query, k_ref[: (block + 1) * BLOCK, :])

    items = [(block, head) for block in range(length // BLOCK) for head in range(2)]
    ahead = score(*items[0])
    result = None
    total = None
    for spot, (block, head) in enumerate(items):
        cut = slice(block * BLOCK, (block + 1) * BLOCK)
        seen = (block + 1) * BLOCK
        scores = ahead
        if spot + 1 < len(items):
            ahead = score(*items[spot + 1])
        top = jnp.max(scores, axis=1, keepdims=True)
        weights = jnp.exp(scores - top).astype(bf16)
        both = dot_nn(weights, wide_ref[:seen, :])
        summed = both[:, 128:]
        out = both[:, :128] / summed
        log_total = top + jnp.log(summed)
        if head == 0:
            result, total = out, log_total
            continue
        result = jnp.where(lane < HEAD, result, out)
        total = jnp.where(lane < HEAD, total, log_total)
        out_ref[cut, :] = result.astype(bf16)
        turned = jnp.transpose(total)
        total_ref[0, 0:1, cut] = turned[0:1, :]
        total_ref[0, 1:2, cut] = turned[HEAD : HEAD + 1, :]


def attend(queries, keys, values):
    length, width = queries.shape
    pair = pl.BlockSpec((length, 128), lambda i: (0, i))
    return pl.pallas_call(
        attend_body,
        grid=(PAIRS,),
        in_specs=[pair] * 3,
        out_specs=[pair, pl.BlockSpec((1, 2, length), lambda i: (i, 0, 0))],
        out_shape=[shape((length, width), bf16), shape((PAIRS, 2, length), f32)],
        scratch_shapes=[pltpu.VMEM((length, 256), bf16)],
        compiler_params=params(),
        cost_estimate=cost(8 * length * length * width, 8 * length * width, LIGHT),
        name="attend",
    )(queries, keys, values)


def mix_body(
    mine_ref,
    attended_ref,
    weight_ref,
    tokens_ref,
    cot_ref,
    small_ref,
    prev_ref,
    routes_ref,
    trow_ref,
    residual_ref,
    normed_ref,
    gates_ref,
    zero_ref,
    *rest,
):
    pieces = rest[:EXPERTS]
    kept, logits_ref, rows_all, sems = rest[EXPERTS:]
    length = kept.shape[0]
    steps = length // ROWS
    step = pl.program_id(0)

    @pl.when(step < steps)
    def _():
        residual = tokens_ref[...].astype(f32) + dot_nn(attended_ref[...], weight_ref[...])
        residual_ref[...] = residual.astype(bf16)
        inverse = lax.rsqrt(jnp.mean(residual * residual, axis=1, keepdims=True) + epsilon)
        normed = (residual * inverse * small_ref[15:16, :]).astype(bf16)
        normed_ref[...] = normed
        kept[pl.ds(pl.multiple_of(step * ROWS, ROWS), ROWS), :] = normed
        small = small_ref[...].astype(bf16)
        cot = cot_ref[...]
        along = jnp.sum(cot.astype(f32) * normed.astype(f32), axis=1, keepdims=True)
        along = jnp.transpose(jnp.broadcast_to(along, (ROWS, 128)))[0:16]
        constant = dot_nt(small, cot)
        line = iota((16, ROWS), 0)
        where = pl.ds(pl.multiple_of(step * ROWS, ROWS), ROWS)
        zero_ref[:, where] = jnp.where(
            line == EXPERTS + 1,
            along,
            jnp.where(
                line == EXPERTS + 2,
                constant[12:13, :],
                jnp.where(line == EXPERTS + 3, constant[13:14, :], 0.0),
            ),
        )
        logits_ref[:, where] = dot_nt(small, normed)

    @pl.when(step == steps)
    def _():
        all_ids = EXPERTS + ZEROS
        logits = logits_ref[0:all_ids, :] + prev_ref[...]
        line = iota((all_ids, length), 0)
        id0 = routes_ref[0:1, :]
        id1 = routes_ref[1:2, :]
        one = jnp.sum(jnp.where(line == id0, logits, 0.0), axis=0, keepdims=True)
        two = jnp.sum(jnp.where(line == id1, logits, 0.0), axis=0, keepdims=True)
        top = jnp.maximum(one, two)
        one = jnp.exp(one - top)
        two = jnp.exp(two - top)
        scale = 1.0 / (one + two)
        gate0 = one * scale
        gate1 = two * scale

        def gate_of(expert):
            return jnp.where(id0 == expert, gate0, jnp.where(id1 == expert, gate1, 0.0))

        line8 = iota((8, length), 0)
        gates = jnp.where(line8 == 0, gate0, jnp.where(line8 == 1, gate1, 0.0))
        for offset in range(1, ZEROS):
            expert = EXPERTS + offset
            own = jnp.where(id0 == expert, gate0, jnp.where(id1 == expert, gate1, 0.0))
            gates = jnp.where(line8 == 1 + offset, own, gates)
        gates_ref[...] = gates
        targets = (trow_ref[0:1, :], trow_ref[1:2, :])
        chosen = one_hot(targets, 0, GROUP, length, 0)
        picked = dot_nn(chosen, kept[...]).astype(bf16)
        rows_all[...] = picked.reshape(EXPERTS, SLOTS, picked.shape[1])
        line16 = iota((16, length), 0)
        expert_of = line16 & (EXPERTS - 1)
        own = jnp.where(id0 == expert_of, gate0, jnp.where(id1 == expert_of, gate1, 0.0))
        high = own.astype(bf16).astype(f32)
        both = jnp.where(line16 < EXPERTS, high, own - high)
        scalars = dot_nt(both.astype(bf16), chosen)
        for expert in range(EXPERTS):
            shift = expert * SLOTS
            turned = pltpu.roll(scalars, GROUP - shift, 1) if shift else scalars
            put_scalars(
                rows_all,
                expert,
                turned[expert : expert + 1, :TILE],
                turned[EXPERTS + expert : EXPERTS + expert + 1, :TILE],
            )
        copies = [
            pltpu.make_async_copy(rows_all.at[mine_ref[0] ^ index], piece, sems.at[index])
            for index, piece in enumerate(pieces)
        ]
        for copy in copies:
            copy.start()
        for copy in copies:
            copy.wait()


def put_scalars(target, index, high, low):
    line = iota((16, TILE), 0)
    lane = iota((16, TILE), 1)
    extra = jnp.where(line == 8, high, jnp.where(line == 9, low, 0.0))
    extra = jnp.where(lane < SLOTS, extra, 0.0)
    last = target[index, SCALAR_ROWS:, :TILE].astype(f32)
    target[index, SCALAR_ROWS:, :TILE] = (last + extra).astype(bf16)


def take_scalars(tile):
    turned = jnp.transpose(tile.astype(f32))[:SLOTS]
    return turned[:, 8:9], turned[:, 9:10]


def mix(mine, attended, weight, tokens, cot, small, prev_row, routes_row, trow):
    length, width = tokens.shape
    steps = length // ROWS
    tile = rows(ROWS, width, steps)
    return pl.pallas_call(
        mix_body,
        grid=(steps + 1,),
        in_specs=[
            SCALAR,
            tile,
            full(weight.shape),
            tile,
            tile,
            full(small.shape),
            full(prev_row.shape),
            full((2, length)),
            full((8, length)),
        ],
        out_specs=[tile, tile, full((8, length)), full((16, length))]
        + [WHOLE] * EXPERTS,
        out_shape=[
            shape((length, width), bf16),
            shape((length, width), bf16),
            shape((8, length), f32),
            shape((16, length), f32),
        ]
        + [shape((SLOTS, width), bf16)] * EXPERTS,
        scratch_shapes=[
            pltpu.VMEM((length, width), bf16),
            pltpu.VMEM((16, length), f32),
            pltpu.VMEM((EXPERTS, SLOTS, width), bf16),
            pltpu.SemaphoreType.DMA((EXPERTS,)),
        ],
        compiler_params=params(),
        cost_estimate=cost(
            2 * length * width * width + 2 * GROUP * length * width, 18 * length * width, LIGHT),
        name="mix",
    )(mine, attended, weight, tokens, cot, small, prev_row, routes_row, trow)


def expert_body(group, chained, mine_ref, *refs):
    count = len(group)
    incoming = refs[:count]
    cot_all, weight_ref = refs[count : count + 2]
    refs = refs[count + 2 + chained :]
    hidden_ref, gate_ref, up_ref, scaled_ref, sent_ref = refs[:5]
    back = refs[5 : 5 + count]
    (
        rows_all,
        cot,
        sent,
        hidden_all,
        grads_all,
        down_all,
        in_all,
        gate_col,
        sems,
    ) = refs[5 + count :]
    step = pl.program_id(0)
    last = pl.num_programs(0) - 1
    width = rows_all.shape[1]
    part = hidden_ref.shape[1]
    inner = hidden_all.shape[1]
    deep = count * SLOTS

    @pl.when(step == 0)
    def _():
        copies = [
            pltpu.make_async_copy(cot_all.at[mine_ref[0] ^ index], cot.at[place_in], sems.at[place_in])
            for place_in, index in enumerate(group)
        ]
        for copy in copies:
            copy.start()
        for index in range(count):
            cut = slice(index * SLOTS, (index + 1) * SLOTS)
            rows_all[cut, :] = incoming[index][...]
            high, low = take_scalars(incoming[index][SCALAR_ROWS:, :TILE])
            gate_col[cut, :] = jnp.broadcast_to(high + low, (SLOTS, 128))
        for copy in copies:
            copy.wait()
        for index in range(count):
            cut = slice(index * SLOTS, (index + 1) * SLOTS)
            scaled_ref[cut, :] = (gate_col[cut, 0:1] * cot[index].astype(f32)).astype(bf16)

    value = rows_all[...]
    scaled = scaled_ref[...]
    several = weight_ref.shape[0]
    part = part // several
    products = [
        (
            dot_nn(value, weight_ref[index, 0]),
            dot_nn(value, weight_ref[index, 1]),
            dot_nn(scaled, weight_ref[index, 2]),
        )
        for index in range(several)
    ]
    for index, (gate, up, grad_hidden) in enumerate(products):
        sigmoid = 1.0 / (1.0 + jnp.exp(-gate))
        active = gate * sigmoid
        hidden = (active * up).astype(bf16)
        grad_up = (grad_hidden * active).astype(bf16)
        grad_gate = (grad_hidden * up * (sigmoid + active * (1.0 - sigmoid))).astype(bf16)
        own = slice(index * part, (index + 1) * part)
        first = (step * several + index) * part
        where = pl.ds(pl.multiple_of(first, part), part)
        behind = pl.ds(pl.multiple_of(inner + first, part), part)
        hidden_ref[:, own] = hidden
        gate_ref[:, own] = grad_gate
        up_ref[:, own] = grad_up
        hidden_all[:, where] = hidden
        grads_all[:, where] = grad_gate
        grads_all[:, behind] = grad_up
        in_all[:, where] = weight_ref[index, 0]
        in_all[:, behind] = weight_ref[index, 1]
        down_all[:, where] = weight_ref[index, 2]

    @pl.when(step == last)
    def _():
        column = gate_col[:, 0:1]
        along = None
        for start in range(0, width, TILE):
            cut = slice(start, start + TILE)
            produced = dot_nt(hidden_all[...], down_all[cut, :]).astype(bf16).astype(f32)
            sent[:, :, cut] = (produced * column).astype(bf16).reshape(count, SLOTS, TILE)
            term = jnp.sum(
                produced * cot[:, :, cut].reshape(deep, TILE).astype(f32), axis=1, keepdims=True
            )
            along = term if along is None else along + term
        copies = [
            pltpu.make_async_copy(
                sent.at[place_in], sent_ref.at[mine_ref[0] ^ index], sems.at[place_in]
            )
            for place_in, index in enumerate(group)
        ]
        for copy in copies:
            copy.start()
        for start in range(0, width, TILE):
            cut = slice(start, start + TILE)
            grads = dot_nt(grads_all[...], in_all[cut, :]).astype(bf16)
            for index in range(count):
                own = grads[index * SLOTS : (index + 1) * SLOTS]
                if start == 0:
                    scalar = along[index * SLOTS : (index + 1) * SLOTS]
                    scalar = jnp.broadcast_to(scalar, (SLOTS, 128))
                    spare = jnp.zeros((TILE - SLOTS, 128), f32)
                    scalar = jnp.transpose(jnp.concatenate([scalar, spare], axis=0))[0:16]
                    high = scalar.astype(bf16).astype(f32)
                    line = iota((16, TILE), 0)
                    extra = jnp.where(line == 8, high, jnp.where(line == 9, scalar - high, 0.0))
                    back[index][:SCALAR_ROWS, cut] = own[:SCALAR_ROWS]
                    last_rows = own[SCALAR_ROWS:].astype(f32) + extra
                    back[index][SCALAR_ROWS:, cut] = last_rows.astype(bf16)
                else:
                    back[index][:, cut] = own
        for copy in copies:
            copy.wait()


def expert_rows(group, mine, incoming, cotangents, weight, sent):
    count = len(group)
    width = incoming[0].shape[1]
    blocks, _, _, part = weight.shape
    inner = blocks * part
    deep = count * SLOTS
    chained = len(sent)
    several = 2 if blocks % 2 == 0 else 1
    block = pl.BlockSpec((deep, several * part), lambda i: (0, i))
    wide = shape((deep, inner), bf16)
    piece = full((SLOTS, width))
    return pl.pallas_call(
        functools.partial(expert_body, group, chained),
        grid=(blocks // several,),
        in_specs=[SCALAR]
        + [piece] * count
        + [WHOLE, pl.BlockSpec((several, 3, width, part), lambda i: (i, 0, 0, 0))]
        + [WHOLE] * chained,
        out_specs=[block, block, block, full((deep, width)), WHOLE] + [piece] * count,
        out_shape=[wide, wide, wide, shape((deep, width), bf16)]
        + [shape((EXPERTS, SLOTS, width), bf16)]
        + [shape((SLOTS, width), bf16)] * count,
        input_output_aliases={count + 3: 4} if chained else {},
        scratch_shapes=[
            pltpu.VMEM((deep, width), bf16),
            pltpu.VMEM((count, SLOTS, width), bf16),
            pltpu.VMEM((count, SLOTS, width), bf16),
            pltpu.VMEM((deep, inner), bf16),
            pltpu.VMEM((deep, 2 * inner), bf16),
            pltpu.VMEM((width, inner), bf16),
            pltpu.VMEM((width, 2 * inner), bf16),
            pltpu.VMEM((deep, 128), f32),
            pltpu.SemaphoreType.DMA((count,)),
        ],
        compiler_params=params(),
        cost_estimate=cost(12 * deep * width * inner, 6 * width * inner + 6 * deep * inner),
        name="expert_rows",
    )(mine, *incoming, cotangents, weight, *sent)


def weights_body(counts, *refs):
    total = sum(counts)
    groups = len(counts)
    incoming = refs[:total]
    scaled = refs[total : total + groups]
    wide = refs[total + groups : total + 4 * groups]
    refs = refs[total + 4 * groups :]
    out_ref = refs[0]
    turned = refs[1:]
    step = pl.program_id(0)

    @pl.when(step == 0)
    def _():
        start = 0
        for group, count in enumerate(counts):
            value = jnp.concatenate(
                [incoming[start + index][...] for index in range(count)], axis=0
            )
            turned[2 * group][...] = jnp.transpose(value)
            turned[2 * group + 1][...] = jnp.transpose(scaled[group][...])
            start += count

    for which in range(3):
        result = None
        for group in range(groups):
            hidden, grad_gate, grad_up = wide[3 * group : 3 * group + 3]
            left = turned[2 * group + (1 if which == 2 else 0)]
            term = dot_nn(left[...], (grad_gate, grad_up, hidden)[which][...])
            result = term if result is None else result + term
        out_ref[0, which] = result.astype(bf16)


def expert_weights(incoming, scaled, wide, blocks):
    width = incoming[0].shape[1]
    inner = wide[0].shape[1]
    part = inner // blocks
    depths = [block.shape[0] for block in scaled]
    in_specs = [full((SLOTS, width))] * len(incoming)
    in_specs += [full((deep, width)) for deep in depths]
    scratch = []
    for deep in depths:
        in_specs += [pl.BlockSpec((deep, part), lambda i: (0, i))] * 3
        scratch += [pltpu.VMEM((width, deep), bf16)] * 2
    return pl.pallas_call(
        functools.partial(weights_body, tuple(deep // SLOTS for deep in depths)),
        grid=(blocks,),
        in_specs=in_specs,
        out_specs=pl.BlockSpec((1, 3, width, part), lambda i: (i, 0, 0, 0)),
        out_shape=shape((blocks, 3, width, part), bf16),
        scratch_shapes=scratch,
        compiler_params=params(),
        cost_estimate=cost(
            6 * GROUP * width * inner, 6 * width * inner + 6 * GROUP * inner, FILL
        ),
        name="expert_weights",
    )(*incoming, *scaled, *wide)


def dealt(height, parts, width, split_of):
    chips, subs = split_of
    return (chips, parts, height // (chips * subs), width)


def deal(place_ref, source, keep_ref, give_ref):
    chips, parts, deep, width = keep_ref.shape
    subs = source.shape[0] // (chips * deep)
    for chip in range(chips):
        for other, target in enumerate((keep_ref, give_ref)[:subs]):
            start = ((place_ref[0] ^ chip) * subs + (place_ref[1] ^ other)) * deep
            block = source[pl.ds(pl.multiple_of(start, 16), deep), :]
            for part in range(parts):
                target[chip, part] = block[:, part * width : (part + 1) * width]


def return_body(
    place_ref,
    tcol_ref,
    routes_ref,
    gates_ref,
    zero_ref,
    small_ref,
    weight_ref,
    residual_ref,
    normed_ref,
    cot_ref,
    attended_ref,
    *rest,
):
    pieces = rest[:EXPERTS]
    logit_ref, grad_res_ref, grad_att_ref, delta_ref, keep_ref, give_ref = rest[
        EXPERTS : EXPERTS + 6
    ]
    out_sum, extra_sum, grads_all, scalars_all, back_all, sems = rest[EXPERTS + 6 :]
    step = pl.program_id(0)
    width = residual_ref.shape[1]
    id0 = routes_ref[0:1, :]
    id1 = routes_ref[1:2, :]
    line = iota((16, ROWS), 0)

    @pl.when(step == 0)
    def _():
        copies = [
            pltpu.make_async_copy(piece, back_all.at[place_ref[2] ^ index], sems.at[index])
            for index, piece in enumerate(pieces)
        ]
        for copy in copies:
            copy.start()
        for copy in copies:
            copy.wait()
        lane = iota((SLOTS, 128), 1)
        for expert in range(EXPERTS):
            high, low = take_scalars(back_all[expert, SCALAR_ROWS:, :TILE])
            spot = jnp.where(lane == expert, high, jnp.where(lane == EXPERTS + expert, low, 0.0))
            scalars_all[expert * SLOTS : (expert + 1) * SLOTS, :] = spot.astype(bf16)

    chosen = one_hot((tcol_ref[:, 0:1], tcol_ref[:, 1:2]), 0, GROUP, ROWS, 1)
    from_rows = dot_nn(chosen, back_all[...].reshape(GROUP, width))
    scalars = jnp.transpose(dot_nn(chosen, scalars_all[...]))
    through = jnp.concatenate(
        [scalars[:EXPERTS] + scalars[EXPERTS : 2 * EXPERTS], zero_ref[EXPERTS:]], axis=0
    )
    gate0 = gates_ref[0:1, :]
    gate1 = gates_ref[1:2, :]
    grad0 = jnp.sum(jnp.where(line == id0, through, 0.0), axis=0, keepdims=True)
    grad1 = jnp.sum(jnp.where(line == id1, through, 0.0), axis=0, keepdims=True)
    mean = gate0 * grad0 + gate1 * grad1
    chosen0 = gate0 * (grad0 - mean)
    chosen1 = gate1 * (grad1 - mean)
    logit = jnp.where(line == id0, chosen0, jnp.where(line == id1, chosen1, 0.0))
    logit_ref[...] = logit[: EXPERTS + ZEROS]
    logit_high, logit_low = split(logit)
    small = small_ref[...].astype(bf16)
    both = jnp.concatenate([logit_high.astype(f32), logit_low.astype(f32)], axis=0).astype(bf16)
    twice = jnp.concatenate([small_ref[...], small_ref[...]], axis=0).astype(bf16)
    grad_normed = dot_tn(both, twice)
    grad_normed += from_rows
    cot = cot_ref[...]
    cot_wide = cot.astype(f32)
    gate_cols = jnp.transpose(gates_ref[...])
    grad_normed += gate_cols[:, 2:3] * cot_wide
    residual = residual_ref[...].astype(f32)
    gain = small_ref[15:16, :]
    inverse = lax.rsqrt(jnp.mean(residual * residual, axis=1, keepdims=True) + epsilon)
    scaled = grad_normed * gain
    spread = jnp.mean(scaled * residual, axis=1, keepdims=True)
    grad_residual = cot_wide + inverse * scaled - residual * (inverse * inverse * inverse * spread)
    grad_low = grad_residual.astype(bf16)
    grad_res_ref[...] = grad_low
    grad_att = dot_nt(grad_low, weight_ref[...]).astype(bf16)
    grad_att_ref[...] = grad_att
    attended = attended_ref[...]
    product = (grad_att.astype(f32) * attended.astype(f32)).astype(bf16)
    head_of = (iota((16, width), 1) >> 6) == iota((16, width), 0)
    delta = dot_nt(mark(head_of), product)
    for pair in range(PAIRS):
        delta_ref[pair] = delta[2 * pair : 2 * pair + 2, :]
    out_term = dot_tn(attended, grad_low)
    grad_gain = jnp.sum(grad_normed * residual * inverse, axis=0, keepdims=True)
    normed = normed_ref[...]
    router_term = dot_nn(logit_high, normed) + dot_nn(logit_low, normed)
    const0 = gates_ref[3:4, :]
    const1 = gates_ref[4:5, :]
    weights = jnp.where(line == 12, const0, jnp.where(line == 13, const1, 0.0))
    const_high, const_low = split(weights)
    const_term = dot_nn(const_high, cot) + dot_nn(const_low, cot)
    extra = router_term + const_term
    extra = jnp.where(iota((16, width), 0) == 15, grad_gain, extra)

    @pl.when(step == 0)
    def _():
        out_sum[...] = out_term
        extra_sum[...] = jnp.zeros_like(extra_sum)
        extra_sum[0:16, :] = extra

    @pl.when(step > 0)
    def _():
        out_sum[...] += out_term
        extra_sum[0:16, :] += extra

    @pl.when(step == pl.num_programs(0) - 1)
    def _():
        small_grads = jnp.transpose(extra_sum[...]).astype(bf16)
        grads_all[:, :width] = out_sum[...].astype(bf16)
        grads_all[:, width:] = small_grads
        deal(place_ref, grads_all, keep_ref, give_ref)


def come_back(
    place_of,
    tcol,
    routes_row,
    gates,
    zero,
    small,
    weight,
    residual,
    normed,
    cot,
    attended,
    pieces,
    split_of,
):
    length, width = cot.shape
    steps = length // ROWS
    tile = rows(ROWS, width)
    dims = dealt(width, 1, width + 128, split_of)
    all_ids = EXPERTS + ZEROS
    return pl.pallas_call(
        return_body,
        grid=(steps,),
        in_specs=[
            SCALAR,
            rows(ROWS, 8),
            columns(2, ROWS),
            columns(8, ROWS),
            columns(16, ROWS),
            full(small.shape),
            full(weight.shape),
            tile,
            tile,
            tile,
            tile,
        ]
        + [WHOLE] * EXPERTS,
        out_specs=[
            columns(all_ids, ROWS),
            tile,
            tile,
            pl.BlockSpec((PAIRS, 2, ROWS), lambda i: (0, 0, i)),
            full(dims),
            full(dims),
        ],
        out_shape=[
            shape((all_ids, length), f32),
            shape((length, width), bf16),
            shape((length, width), bf16),
            shape((PAIRS, 2, length), f32),
            shape(dims, bf16),
            shape(dims, bf16),
        ],
        scratch_shapes=[
            pltpu.VMEM((width, width), f32),
            pltpu.VMEM((128, width), f32),
            pltpu.VMEM((width, width + 128), bf16),
            pltpu.VMEM((GROUP, 128), bf16),
            pltpu.VMEM((EXPERTS, SLOTS, width), bf16),
            pltpu.SemaphoreType.DMA((EXPERTS,)),
        ],
        compiler_params=params(),
        cost_estimate=cost(
            4 * length * width * width + 2 * GROUP * length * width, 18 * length * width, 30),
        name="come_back",
    )(
        place_of,
        tcol,
        routes_row,
        gates,
        zero,
        small,
        weight,
        residual,
        normed,
        cot,
        attended,
        *pieces,
    )


def attend_back_body(
    place_ref,
    q_ref,
    k_ref,
    v_ref,
    grad_ref,
    total_ref,
    delta_ref,
    cos_ref,
    sin_ref,
    normed_ref,
    grads_ref,
    keep_ref,
    give_ref,
    query_turned,
    grad_turned,
    key_turned,
    value_turned,
    query_sum,
    normed_turned,
    weight_grads,
):
    @pl.when(pl.program_id(0) == 0)
    def _():
        normed_turned[...] = jnp.transpose(normed_ref[...])

    length = q_ref.shape[0]
    cosine = cos_ref[...]
    sine = sin_ref[...]
    lane = iota((BLOCK, 128), 1)
    query_turned[...] = jnp.transpose(q_ref[...])
    grad_turned[...] = jnp.transpose(grad_ref[...])
    scalars = [total_ref[0], delta_ref[0], jnp.zeros((4, length), f32)]
    scalars = jnp.transpose(jnp.concatenate(scalars, axis=0))

    def products(block, head):
        cut = slice(block * BLOCK, (block + 1) * BLOCK)
        mine = (lane < HEAD) if head == 0 else (lane >= HEAD)
        key = jnp.where(mine, k_ref[cut, :], jnp.zeros((BLOCK, 128), bf16))
        value = jnp.where(mine, v_ref[cut, :], jnp.zeros((BLOCK, 128), bf16))
        scores = dot_nt(q_ref[block * BLOCK :, :], key)
        return key, scores, dot_nt(grad_ref[block * BLOCK :, :], value)

    items = [(block, head) for block in range(length // BLOCK) for head in range(2)]
    ahead = products(*items[0])
    query_term = None
    for spot, (block, head) in enumerate(items):
        start = block * BLOCK
        cut = slice(start, start + BLOCK)
        line = slice(head * HEAD, (head + 1) * HEAD)
        key, scores, grad_weights = ahead
        if spot + 1 < len(items):
            ahead = products(*items[spot + 1])
        weights = jnp.exp(scores - scalars[start:, head : head + 1])
        grad_scores = weights * (grad_weights - scalars[start:, head + 2 : head + 3])
        grad_scores = grad_scores.astype(bf16)
        term = dot_nn(grad_scores, key)
        value_turned[line, cut] = dot_nn(grad_turned[line, start:], weights.astype(bf16))
        key_turned[line, cut] = dot_nn(query_turned[line, start:], grad_scores)
        if head == 0:
            query_term = term
        elif block == 0:
            query_sum[...] = query_term + term
        else:
            query_sum[start:, :] += query_term + term
    grad_key = jnp.transpose(key_turned[...]).astype(bf16).astype(f32)
    grads_ref[:, 128:256] = turn(grad_key, cosine, -sine).astype(bf16)
    grads_ref[:, 256:] = jnp.transpose(value_turned[...]).astype(bf16)
    grad_query = (query_sum[...] * 0.125).astype(bf16).astype(f32)
    grads_ref[:, :128] = turn(grad_query, cosine, -sine).astype(bf16)
    weight_grads[...] = dot_nn(normed_turned[...], grads_ref[...]).astype(bf16)
    deal(place_ref, weight_grads, keep_ref, give_ref)


def attend_back(
    first, count, place_of, queries, keys, values, grad, total, delta, cosine, sine, normed, split_of
):
    length, width = queries.shape
    pair = pl.BlockSpec((length, 128), lambda i: (0, i + first))
    line = pl.BlockSpec((1, 2, length), lambda i: (i + first, 0, 0))
    chips, parts, deep, across = dealt(width, 3, 128 * count, split_of)
    block = pl.BlockSpec((chips, parts, deep, 128), lambda i: (0, 0, 0, i))
    dims = shape((chips, parts, deep, across), bf16)
    return pl.pallas_call(
        attend_back_body,
        grid=(count,),
        in_specs=[SCALAR]
        + [pair] * 4
        + [line, line, full((length, 128)), full((length, 128)), full((length, width))],
        out_specs=[columns(length, 384), block, block],
        out_shape=[shape((length, 384 * count), bf16), dims, dims],
        scratch_shapes=[
            pltpu.VMEM((128, length), bf16),
            pltpu.VMEM((128, length), bf16),
            pltpu.VMEM((128, length), f32),
            pltpu.VMEM((128, length), f32),
            pltpu.VMEM((length, 128), f32),
            pltpu.VMEM((width, length), bf16),
            pltpu.VMEM((width, 384), bf16),
        ],
        compiler_params=params(),
        cost_estimate=cost(
            26 * length * length * 128 * count, 14 * length * 128 * count, LATE),
        name="attend_back",
    )(place_of, queries, keys, values, grad, total, delta, cosine, sine, normed)


def tokens_grad_body(first_ref, second_ref, weight_ref, tokens_ref, grad_res_ref, small_ref, out_ref):
    width = tokens_ref.shape[1]
    grad_normed = None
    for group, ref in enumerate((first_ref, second_ref)):
        pairs = ref.shape[1] // 384
        for part in range(3):
            start = part * width + group * pairs * 128
            grads = jnp.concatenate(
                [
                    ref[:, pair * 384 + part * 128 : pair * 384 + part * 128 + 128]
                    for pair in range(pairs)
                ],
                axis=1,
            )
            term = dot_nt(grads, weight_ref[:, start : start + pairs * 128])
            grad_normed = term if grad_normed is None else grad_normed + term
    value = tokens_ref[...].astype(f32)
    inverse = lax.rsqrt(jnp.mean(value * value, axis=1, keepdims=True) + epsilon)
    scaled = grad_normed * small_ref[14:15, :]
    spread_of = jnp.mean(scaled * value, axis=1, keepdims=True)
    grad = inverse * scaled - value * (inverse * inverse * inverse * spread_of)
    out_ref[...] = grad_res_ref[...].astype(f32) + grad


def tokens_grad(grads, weight, tokens, grad_res, small):
    length, width = tokens.shape
    tile = rows(ROWS, width)
    wide = grads[0].shape[1]
    return pl.pallas_call(
        tokens_grad_body,
        grid=(length // ROWS,),
        in_specs=[rows(ROWS, wide)] * 2
        + [full(weight.shape), tile, tile, full(small.shape)],
        out_specs=tile,
        out_shape=shape((length, width), f32),
        compiler_params=params(),
        cost_estimate=cost(6 * length * width * width, 16 * length * width, LATE),
        name="tokens_grad",
    )(*grads, weight, tokens, grad_res, small)


def output_body(
    tcol_ref, gates_ref, small_ref, residual_ref, normed_ref, block_ref, out_ref
):
    gates = gates_ref[...]
    line = iota(gates.shape, 0)
    gate_cols = jnp.transpose(gates)
    consts = jnp.where((line == 3) | (line == 4), gates, 0.0)
    high, low = split(consts)
    vectors = jnp.where(iota((8, small_ref.shape[1]), 0) == 3, small_ref[12:13, :], 0.0)
    vectors = jnp.where(
        iota((8, small_ref.shape[1]), 0) == 4, small_ref[13:14, :], vectors
    )
    both = jnp.concatenate([high.astype(f32), low.astype(f32)], axis=0).astype(bf16)
    twice = jnp.concatenate([vectors, vectors], axis=0).astype(bf16)
    total = residual_ref[...].astype(f32) + dot_tn(both, twice)
    total += gate_cols[:, 2:3] * normed_ref[...].astype(f32)
    chosen = one_hot((tcol_ref[:, 0:1], tcol_ref[:, 1:2]), 0, GROUP, ROWS, 1)
    total += dot_nn(chosen, block_ref[...].reshape(GROUP, block_ref.shape[2]))
    out_ref[...] = total.astype(bf16)


def output(tcol, gates, small, residual, normed, block):
    length, width = residual.shape
    tile = rows(ROWS, width)
    return pl.pallas_call(
        output_body,
        grid=(length // ROWS,),
        in_specs=[rows(ROWS, 8), columns(8, ROWS), full(small.shape), tile, tile]
        + [full((EXPERTS, SLOTS, width))],
        out_specs=tile,
        out_shape=shape((length, width), bf16),
        compiler_params=params(),
        cost_estimate=cost(2 * GROUP * length * width, 12 * length * width, LATE),
        name="output",
    )(tcol, gates, small, residual, normed, block)


def finish_body(low_ref, high_ref, first_ref, weight_ref, gain_ref, out_ref, gain_out):
    across = low_ref.shape[1] // 3
    weighted = None
    for part in range(3):
        cut = slice(part * across, (part + 1) * across)
        for half in range(2):
            if half:
                grads = low_ref[:, cut].astype(f32) + high_ref[:, cut].astype(f32)
            else:
                grads = first_ref[:, cut]
            place_of = slice((2 * part + half) * across, (2 * part + half + 1) * across)
            out_ref[:, place_of] = grads
            term = jnp.sum(grads * weight_ref[:, place_of].astype(f32), axis=1, keepdims=True)
            weighted = term if weighted is None else weighted + term
    gain_out[...] = weighted / gain_ref[...]


def finish(low, high, first, weight, gain):
    given = (low, high, first, weight, gain)
    return pl.pallas_call(
        finish_body,
        grid=(1,),
        in_specs=[full(value.shape) for value in given],
        out_specs=[full(weight.shape), full(gain.shape)],
        out_shape=[shape(weight.shape, f32), shape(gain.shape, f32)],
        compiler_params=params(),
        cost_estimate=cost(1000, 1000),
        name="finish",
    )(*given)


def local(
    tokens,
    cotangent,
    prev_logits,
    routes,
    priority,
    gain_mix,
    mix_qkv,
    mix_out,
    gain_moe,
    router,
    constants,
    w_gate,
    w_up,
    w_down,
):
    length, width = tokens.shape
    here, _, part = w_gate.shape
    depth = lax.axis_size("expert")
    chips = lax.axis_size("chip")
    z = lax.axis_index("expert").astype(jnp.int32)
    chip = lax.axis_index("chip").astype(jnp.int32)
    sub = lax.axis_index("sub").astype(jnp.int32)
    pairwise = chips == 4 and here == 2
    split_of = (chips, here) if pairwise else (1, 1)
    own = (z * here + sub).astype(jnp.int32)
    mine_of = own.reshape(1)
    spot = (chip, sub) if pairwise else (jnp.int32(0), jnp.int32(0))
    place_of = jnp.stack([*spot, own])
    members = [(a, b) for a in range(depth) for b in range(here)]

    def partner(index, value):
        if index == 0:
            return value
        moves = []
        for source, (a, b) in enumerate(members):
            c, d = members[source ^ index]
            moves += [
                ((a * chips + i) * here + b, (c * chips + i) * here + d) for i in range(chips)
            ]
        return lax.ppermute(value, ("expert", "chip", "sub"), moves)

    def trade(value, axis, size, index):
        return lax.ppermute(value, axis, [(i, i ^ index) for i in range(size)])

    def exchange(value):
        return lax.all_to_all(value, ("expert", "sub"), split_axis=0, concat_axis=0, tiled=True)

    features = mix_qkv.shape[0]
    extra = jnp.concatenate(
        [router, constants, gain_mix[:, None], gain_moe[:, None]], axis=1
    )
    extra = jnp.pad(extra, ((0, 0), (0, 128 - extra.shape[1])))
    packed = jnp.concatenate([mix_qkv, extra, mix_out], axis=1)
    routes_row = routes.T
    order_row = priority.reshape(length, 2).T
    trow, tcol, grads_out = place(routes_row, order_row, cotangent)
    cot_in = exchange(grads_out)

    if pairwise:
        near = [trade(packed, "chip", chips, index) for index in (1, 2)]
    else:
        near = [packed]

    def of_expert(index):
        return jnp.stack(
            [lax.dynamic_index_in_dim(w, index, 0, keepdims=False) for w in (w_gate, w_up, w_down)]
        )

    keep = of_expert(sub)
    if here == 1:
        mine = keep[None]
    else:
        give = of_expert(1 - sub)
        mine = jnp.stack([keep, trade(give, "sub", here, 1)], axis=0)
    weight = lax.all_gather(mine, "chip", axis=0, tiled=True)
    count = weight.shape[0]
    if part < 256:
        join = 256 // part
        weight = weight.reshape(count // join, join, 3, width, part)
        weight = weight.transpose(0, 2, 3, 1, 4).reshape(count // join, 3, width, 256)

    if pairwise:
        near = [after(piece, trow, mine) for piece in near]
        half = features // 2
        far = [
            trade(near[1][:half], "chip", chips, 1),
            trade(near[0][half:], "chip", chips, 2),
        ]
        pieces = [packed, *near, *far]
        spots = [chip, chip ^ 1, chip ^ 2, chip ^ 3, chip ^ 3]
        lower = [0, 0, 0, 0, half]
        pieces += [trade(piece, "sub", here, 1) for piece in pieces]
        where = jnp.stack(
            [(spot * here + sub) * features + low for spot, low in zip(spots, lower)]
            + [(spot * here + (sub ^ 1)) * features + low for spot, low in zip(spots, lower)]
        )
    else:
        pieces = [lax.all_gather(packed, ("chip", "sub"), axis=0, tiled=True)]
        where = jnp.zeros((1,), jnp.int32)

    cosine, sine = rotary(length)
    outs = project(tokens, pieces, where, cosine, sine)
    queries, keys, values, normed_one, small, qkv, out_w = outs
    attended, log_total = attend(queries, keys, values)
    outs = mix(mine_of, attended, out_w, tokens, cotangent, small, prev_logits.T, routes_row, trow)
    residual, normed_two, gates, zero = outs[:4]
    leaving = outs[4:]
    rows_in = [None] * EXPERTS
    returned = [None] * EXPERTS
    near = GROUPS[0][1:]
    for index in GROUPS[0]:
        rows_in[index] = partner(index, leaving[index])

    def cross(group, *others):
        crossing = all_after([leaving[index] for index in group], *others)
        for index, block in zip(group, crossing):
            rows_in[index] = partner(index, block)

    cross(GROUPS[1], *[rows_in[index] for index in near])

    sent, scaled, wide, ordered = [], [], [], []
    blocks = weight.shape[0]
    for group in GROUPS[:2]:
        incoming = [rows_in[index] for index in group]
        outs = expert_rows(group, mine_of, incoming, cot_in, weight, sent)
        wide += outs[:3]
        scaled.append(outs[3])
        sent = [outs[4]]
        ordered += incoming
        for index, block in zip(group, outs[5:]):
            returned[index] = partner(index, block)
        if group == GROUPS[0]:
            cross(GROUPS[2], outs[3], *[rows_in[index] for index in GROUPS[1]])
    group = GROUPS[2]
    incoming = [rows_in[index] for index in group]
    sent[0] = after(sent[0], *[returned[index] for index in near])
    outs = expert_rows(group, mine_of, incoming, cot_in, weight, sent)
    wide += outs[:3]
    scaled.append(outs[3])
    sent = outs[4]
    ordered += incoming
    grads_w = expert_weights(ordered, scaled, wide, blocks)
    for index, block in zip(group, outs[5:]):
        returned[index] = partner(index, block)
    residual_late = after(residual, grads_w, *[returned[index] for index in GROUPS[1]])

    if part < 256:
        grads_w = grads_w.reshape(count // join, 3, width, join, part)
        grads_w = grads_w.transpose(0, 3, 1, 2, 4).reshape(count, 3, width, part)
    grads_w = lax.psum_scatter(grads_w, "chip", scatter_dimension=0, tiled=True)
    outs = come_back(
        place_of,
        tcol,
        routes_row,
        gates,
        zero,
        small,
        out_w,
        residual_late,
        normed_two,
        cotangent,
        attended,
        returned,
        split_of,
    )
    logit_grad, grad_res, grad_att, delta = outs[:4]
    dealt_out = outs[4:]
    produced = exchange(after(sent, grad_att))

    def flat(block):
        return block.transpose(1, 0, 2).reshape(block.shape[1], -1)

    def over_cores(dealt_parts):
        if not pairwise:
            return [jnp.concatenate([flat(keep[0]) for keep, _ in dealt_parts], axis=1)]
        got = [trade(give, "sub", here, 1) for _, give in dealt_parts]
        sums = []
        for index in range(chips):
            both = [
                flat(keep[index]).astype(f32) + flat(other[index]).astype(f32)
                for (keep, _), other in zip(dealt_parts, got)
            ]
            sums.append(jnp.concatenate(both, axis=1).astype(bf16 if index else f32))
        return sums

    def over_chips(sums):
        if not pairwise:
            axes = ("chip", "sub")
            return lax.psum_scatter(sums[0], axes, scatter_dimension=0, tiled=True).astype(f32)
        total = sums[0]
        for index in range(1, chips):
            total += trade(sums[index], "chip", chips, index).astype(f32)
        return total

    def over_planes(total, index, *beside):
        low = total.astype(bf16)
        other = trade(low, "expert", depth, index)
        return after(low, *beside).astype(f32) + other.astype(f32)

    def back_through(first, normed):
        return attend_back(
            first,
            count,
            place_of,
            queries,
            keys,
            values,
            grad_att,
            log_total,
            delta,
            cosine,
            sine,
            normed,
            split_of,
        )

    count = PAIRS // 2
    grads_a, *dealt_a = back_through(0, normed_one)
    sums_a = over_cores([dealt_a, dealt_out])
    grads_b, *dealt_b = back_through(count, after(normed_one, sums_a[-1]))
    total_a = over_chips([after(sums_a[0], grads_b), *sums_a[1:]])
    dealt_b[1] = after(dealt_b[1], total_a)
    sums_b = over_cores([dealt_b])
    token_grad = tokens_grad([grads_a, grads_b], qkv, tokens, after(grad_res, total_a, sums_b[-1]), small)
    total_b = over_chips([after(sums_b[0], token_grad, produced), *sums_b[1:]])
    low_b = total_b.astype(bf16)
    block_out = output(tcol, gates, small, after(residual, low_b), normed_two, produced)
    index = 1
    while index < depth:
        total_a = over_planes(total_a, index, token_grad if index == 1 else block_out)
        index *= 2
    beside = [block_out, total_a]
    index = 1
    while index < depth // 2:
        total_b = over_planes(total_b, index, *beside)
        beside = []
        index *= 2
    low_b = total_b.astype(bf16)
    high_b = trade(low_b, "expert", depth, index)

    if here == 1:
        grads_w = grads_w[0][:, None].astype(f32)
    else:
        kept = grads_w[0]
        theirs = trade(after(grads_w[1], low_b), "sub", here, 1)
        pair = jnp.stack([kept, theirs], axis=1).astype(f32)
        swapped = jnp.stack([theirs, kept], axis=1).astype(f32)
        grads_w = jnp.where(sub == 0, pair, swapped)
    grads_w = (grads_w[0], grads_w[1], grads_w[2])

    across = 128 * count
    mixed = total_a[:, 3 * across :]
    grad_qkv, grad_gain = finish(
        after(low_b, *grads_w), high_b, total_a, mix_qkv, gain_mix.astype(f32)[:, None]
    )
    grad_gain = grad_gain[:, 0]
    all_ids = EXPERTS + ZEROS
    return (
        block_out,
        token_grad,
        logit_grad.T,
        grad_gain,
        grad_qkv,
        mixed[:, :width],
        mixed[:, width + 15],
        mixed[:, width : width + all_ids],
        mixed[:, width + 12 : width + 14],
        *grads_w,
    )


def solution(mesh):
    depth = mesh.shape["expert"]
    here = EXPERTS // depth
    chips = mesh.shape["shard"] // here
    fine = Mesh(mesh.devices.reshape(depth, chips, here), ("expert", "chip", "sub"))
    shard = ("chip", "sub")
    by_token = P(("expert", "chip", "sub"), None)
    weights = P("expert", None, shard)
    mixer = (P(shard), P(shard, None), P(shard, None), P(shard), P(shard, None), P(shard, None))
    in_specs = (by_token,) * 5 + mixer + (weights,) * 3
    out_specs = (by_token,) * 3 + mixer + (weights,) * 3
    return jax.shard_map(
        local, mesh=fine, in_specs=in_specs, out_specs=out_specs, check_vma=False
    )
```
